512 devices in a mesh: lat: 128 (over x, z, core), lev: 4 (over y).
Axes of the slice: x: 4, y: 4, z: 16, core: 2. Of those that a mesh axis runs over, the one named last changes fastest.
Arguments:
- spec_in: bfloat16 [128, 192, 1280], P('lat', 'lev'), may hold values from -6 to 6
- legendre: bfloat16 [128, 512, 1280], P('lat'), may hold values from -0.15625 to 0.15625
- wavenum: int32 [128], replicated, may hold values from 0 to 1279, as said below
- counts: int32 [512], P('lat'), may hold values from 3856 to 5136, as said below
- quad_weights: float32 [512], P('lat'), may hold values from 1 to 4
- vert_in: float32 [32, 32], P(None, 'lev'), may hold values from -1 to 1
- vert_out: float32 [32, 32], P('lev'), may hold values from -1 to 1
- mode_rates: float32 [32], replicated, may hold values from 0.1 to 10
Outputs:
- spec_out: bfloat16 [128, 192, 1280], P('lat', 'lev')
The draws below stay inside these ranges and needn't reach their ends.
Inputs may be any that keep to these rules, and one draw needn't show every extreme that they name: `wavenum`: 128 distinct wavenumbers below 1280; 0 and 1279 are among them. `counts`: each count is 20 + 4 k for a whole k; the first latitude has 5136 points.
All inputs are finite; a program needn't handle non-finite values.
Results may differ from the reference program's by a relative error of at most 0.0054.
Values may be sent and summed in bfloat16 or wider, within the bound.
A program may use at most 64 MiB of HBM per device.

```python
import math
import jax
import jax.numpy as jnp
from jax import lax

NTRUNC = 1280
PTS = 5136
FIELDS = 3
M_ALL = 128
NLAT = 512
LEV = 32


def draw_wavenum(key, part):
    key = jax.random.fold_in(key, 7)
    key_middle, key_order = jax.random.split(key)
    middle = 1 + jax.random.permutation(key_middle, NTRUNC - 2)[:M_ALL - 2]
    extremes = jnp.array([0, NTRUNC - 1], dtype=jnp.int32)
    chosen = jnp.concatenate([extremes, middle.astype(jnp.int32)])
    return chosen[jax.random.permutation(key_order, M_ALL)].astype(jnp.int32)


def draw_counts(key, part):
    key = jax.random.fold_in(key, 11)
    top_cycle = (PTS - 20) // 4
    cycles = jax.random.randint(key, (NLAT,), 3 * top_cycle // 4, top_cycle + 1)
    cycles = cycles.at[0].set(top_cycle)
    return (20 + 4 * cycles).astype(jnp.int32)


def block_scale(stream_key, extent, cuts, low, largest):
    def one(position, shards_of):
        draws = jax.random.uniform(jax.random.fold_in(jax.random.fold_in(stream_key, 6), position), (shards_of,), jnp.float32, low / len(cuts), largest / len(cuts))
        return jnp.repeat(jnp.exp(draws), extent[position] // shards_of).reshape((-1,) + (1,) * (len(extent) - position - 1))

    loudness = one(*cuts[0])
    for cut in cuts[1:]:
        loudness = loudness * one(*cut)
    return loudness


def centred(stream_key, shape, deviation, bound, cuts=(), held_as=jnp.bfloat16):
    values = jax.random.normal(stream_key, shape, jnp.float32) * deviation
    if len(cuts) > 0:
        values = block_scale(stream_key, shape, cuts, -0.22, 0.18) * values
    return jnp.clip(values, min=-bound, max=bound).astype(held_as)


def setup_inputs(seed: int = 0) -> dict:
    keys = jax.random.split(jax.random.key(seed), 9)
    spec_in = centred(keys[0], (M_ALL, 2 * FIELDS * LEV, NTRUNC), 1.0, 6.0, ((0, 128), (1, 4)))
    legendre = centred(keys[1], (M_ALL, NLAT, NTRUNC), NTRUNC ** -0.5, 0.15625, ((0, 128),))
    wavenum = draw_wavenum(jax.random.fold_in(keys[8], 71), 0)
    counts = draw_counts(jax.random.fold_in(keys[8], 71), 0)
    quad_weights = jnp.clip(jnp.exp(math.log(4.0) - 1.3862944 * jax.random.uniform(keys[4], (NLAT,), jnp.float32) ** block_scale(keys[4], (NLAT,), ((0, 128),), -0.2, 0.2)), 1.0, 4.0)
    vert_in = centred(keys[5], (LEV, LEV), LEV ** -0.5, 1.0, ((1, 4),), jnp.float32)
    vert_out = centred(keys[6], (LEV, LEV), LEV ** -0.5, 1.0, ((0, 4),), jnp.float32)
    mode_rates = jnp.clip(jnp.exp(jax.random.uniform(keys[7], (LEV,), jnp.float32, math.log(0.1), math.log(10.0))), 0.1, 10.0)
    return dict(spec_in=spec_in, legendre=legendre, wavenum=wavenum, counts=counts, quad_weights=quad_weights, vert_in=vert_in, vert_out=vert_out, mode_rates=mode_rates)


full_turn = 2.0 * math.pi

def trig_rows(wavenum, point_count):
    points = jnp.arange(PTS, dtype=jnp.int32)
    phases = wavenum[:, None] * points[None, :] % point_count
    angles = phases.astype(jnp.float32) * (full_turn / point_count.astype(jnp.float32))
    inside = points[None, :] < point_count
    cosine = jnp.where(inside, jnp.cos(angles), 0.0)
    sine_rows = jnp.where(inside, jnp.sin(angles), 0.0)
    return jnp.concatenate([cosine, sine_rows], 0).astype(jnp.bfloat16)

def grid_step(coeffs, wavenum, point_count, weight):
    wave_count = coeffs.shape[0]
    row_count = coeffs.shape[1] // 2
    trig_table = trig_rows(wavenum, point_count)
    paired = coeffs.reshape(wave_count, row_count, 2)
    stacked = jnp.concatenate([paired[:, :, 0], paired[:, :, 1]], 0)
    fields = lax.dot_general(stacked, trig_table, (((0,), (0,)), ((), ())), preferred_element_type=jnp.float32)
    fields = fields * (1.0 / math.sqrt(2 * wave_count))
    levels = fields.reshape(row_count // FIELDS, FIELDS, PTS)
    diverg_grid = levels[:, 0]
    wind_grid = levels[:, 1]
    temp_grid = levels[:, 2]
    tendency = jnp.stack([diverg_grid - wind_grid * temp_grid, wind_grid + diverg_grid * temp_grid, temp_grid - diverg_grid * wind_grid], 1)
    tendency = tendency.reshape(row_count, PTS).astype(jnp.bfloat16)
    spectra = lax.dot_general(tendency, trig_table, (((1,), (1,)), ((), ())), preferred_element_type=jnp.float32)
    factor = weight / jnp.sqrt(point_count.astype(jnp.float32))
    cosine = spectra[:, :wave_count] * factor
    sine_part = -spectra[:, wave_count:] * factor
    return jnp.stack([cosine.T, sine_part.T], 2).reshape(wave_count, 2 * row_count).astype(jnp.bfloat16)

def reference(spec_in, legendre, wavenum, counts, quad_weights, vert_in, vert_out, mode_rates):
    columns = jnp.arange(NTRUNC, dtype=jnp.int32)

    def inverse_one(operands):
        coeffs, table_rows, wave_order = operands
        masked = jnp.where(columns[None, :] >= wave_order, table_rows, jnp.zeros_like(table_rows))
        product = lax.dot_general(coeffs, masked, (((1,), (1,)), ((), ())), preferred_element_type=jnp.float32)
        return product.astype(jnp.bfloat16)
    fourier = lax.map(inverse_one, (spec_in, legendre, wavenum))

    def latitude_one(operands):
        coeffs, point_count, weight = operands
        return grid_step(coeffs, wavenum, point_count, weight)
    returned = lax.map(latitude_one, (fourier.transpose(2, 0, 1), counts, quad_weights))
    returned = returned.transpose(1, 2, 0)

    def direct_one(operands):
        coeffs, table_rows, wave_order = operands
        masked = jnp.where(columns[None, :] >= wave_order, table_rows, jnp.zeros_like(table_rows))
        return jnp.dot(coeffs, masked, preferred_element_type=jnp.float32)
    spectra = lax.map(direct_one, (returned, legendre, wavenum))
    shaped = spectra.reshape(M_ALL, LEV, FIELDS, 2, NTRUNC)
    diverg = shaped[:, :, 0]
    mode_values = jnp.einsum('kl,mlpn->mkpn', vert_in, diverg, precision=lax.Precision.HIGHEST)
    degree = columns.astype(jnp.float32)
    growth = degree * (degree + 1.0) / float(NTRUNC * NTRUNC)
    divisor = 1.0 + mode_rates[:, None] * growth[None, :]
    damped = mode_values / divisor[None, :, None, :]
    solved = jnp.einsum('lk,mkpn->mlpn', vert_out, damped, precision=lax.Precision.HIGHEST)
    result = shaped.at[:, :, 0].set(solved)
    return result.reshape(M_ALL, 2 * FIELDS * LEV, NTRUNC).astype(jnp.bfloat16)
```

```python
import functools
import math

import jax
import jax.numpy as jnp
from jax import lax
from jax.experimental import pallas as pl
from jax.experimental.pallas import tpu as pltpu
from jax.sharding import PartitionSpec as P

PTS = 5136
FIELDS = 3
XS = 4
CORES = 2
LATS = 4
LEVS = 8
LANES = 128
HALF = 64

F32 = jnp.float32
BF16 = jnp.bfloat16
MESH = pl.DeviceIdType.MESH

ROWS_BY_ROWS = (((1,), (1,)), ((), ()))


def dot(a, b):
    return jnp.dot(a, b, preferred_element_type=F32)


def dot_rows(a, b):
    return lax.dot_general(a, b, ROWS_BY_ROWS, preferred_element_type=F32)


def iota(shape, dim):
    return lax.broadcasted_iota(jnp.int32, shape, dim)


def unit(size):
    return jnp.where(iota((size, size), 0) == iota((size, size), 1), 1.0, 0.0).astype(BF16)


def half_up(value):
    return jnp.floor(value + 0.5)


def turn(steps, count, per_count):
    left = steps - half_up(steps * per_count) * count
    x = left * per_count * math.pi
    y = x * x
    s = -1.0 / 39916800
    for term in (1.0 / 362880, -1.0 / 5040, 1.0 / 120, -1.0 / 6, 1.0):
        s = s * y + term
    s = s * x
    c = 1.0 / 479001600
    for term in (-1.0 / 3628800, 1.0 / 40320, -1.0 / 720, 1.0 / 24, -0.5, 1.0):
        c = c * y + term
    return 1.0 - 2.0 * s * s, 2.0 * s * c


def kernel(
    zs, ys, spec_ref, leg_hbm, wav_row, wav_s, counts_s, weights_s, rates_s, vin_ref, vout_ref,
    out_ref,
    leg, spec2, fou, stage, wcol, table, lp, inv, out32,
    s1_out, s1_in, s2_out, s2_in, b2_out, b2_in, b1_out, b1_in, y_out, y_in, v_out, v_in,
    leg_sem, send_sem, recv_sem,
):
    ds = XS * CORES
    waves = ds * zs
    lat_all = waves * LATS
    trunc = spec_ref.shape[2]
    points = table.shape[2]
    levels_all = ys * LEVS
    me = lax.axis_index("lat")
    y = lax.axis_index("lev")
    x = me // (zs * CORES)
    z = (me // CORES) % zs
    core = me % CORES
    d = x * CORES + core

    z_peers = []
    for k in range(1, zs):
        to = (z + k) % zs
        z_peers.append((to, (x * (zs * CORES) + to * CORES + core, y)))
    d_peers = []
    for k in range(1, ds):
        to = (d + k) % ds
        d_peers.append((to, ((to // CORES) * (zs * CORES) + z * CORES + to % CORES, y)))
    y_peers = []
    for k in range(1, ys):
        to = (y + k) % ys
        y_peers.append((to, (me, to)))

    barrier = pltpu.get_barrier_semaphore()
    for _, device in z_peers + d_peers + y_peers:
        pl.semaphore_signal(barrier, inc=1, device_id=device, device_id_type=MESH)

    def send(number, source, arrive, slot, peers):
        pltpu.make_async_copy(source(slot), arrive.at[slot], recv_sem.at[number]).start()
        for to, device in peers:
            pltpu.make_async_remote_copy(
                src_ref=source(to), dst_ref=arrive.at[slot],
                send_sem=send_sem.at[number], recv_sem=recv_sem.at[number],
                device_id=device, device_id_type=MESH,
            ).start()

    def arrived(number, arrive):
        pltpu.make_async_copy(arrive, arrive, recv_sem.at[number]).wait()

    def sent(number, arrive, count):
        part = arrive.at[pl.ds(0, count)]
        pltpu.make_async_copy(part, part, send_sem.at[number]).wait()

    part_rows = lat_all // XS
    loads = []
    for k in range(XS):
        rows = pl.ds(k * part_rows, part_rows)
        loads.append(pltpu.make_async_copy(leg_hbm.at[0, rows], leg.at[rows], leg_sem.at[k]))
        loads[-1].start()

    order = wav_s[me]
    kept = iota((1, trunc), 1) >= order
    columns = spec_ref.shape[1]
    masked = jnp.where(kept, spec_ref[0].astype(F32), 0.0).astype(BF16)
    blank = jnp.zeros((HALF - columns, trunc), BF16)
    spec2[0:columns] = masked
    spec2[columns:HALF] = blank
    spec2[HALF : HALF + columns] = masked
    spec2[HALF + columns :] = blank

    lane = iota((levels_all, 4 * levels_all), 1) % levels_all
    spread = jnp.zeros((levels_all, 4 * levels_all), F32)
    for k in range(LEVS):
        spread = jnp.where(lane == y * LEVS + k, vin_ref[:, k : k + 1], spread)
    v_out[...] = spread

    for k in range(XS):
        loads[k].wait()
        rows = pl.ds(k * part_rows, part_rows)
        fou[rows] = dot_rows(leg[rows], spec2[...])

    first_half = iota((LATS, LANES), 1) < HALF
    for to in range(zs):
        for k in range(XS):
            low = fou[pl.ds(k * part_rows + 8 * to, 4, stride=2)]
            high = fou[pl.ds(k * part_rows + 8 * to + 1, 4, stride=2)]
            stage[pl.ds(to * 4 * XS + 4 * k, 4)] = jnp.where(first_half, low, high)
    s1_out[...] = stage[...].astype(BF16).reshape(s1_out.shape)

    pl.semaphore_wait(barrier, len(z_peers) + len(d_peers) + len(y_peers))
    send(0, lambda slot: s1_out.at[slot], s1_in, z, z_peers)
    send(5, lambda slot: v_out, v_in, y, y_peers)

    place = iota((waves, waves), 0)
    across = iota((waves, waves), 1)
    natural = (place // (CORES * zs)) * (CORES * zs) + (place % zs) * CORES + (place // zs) % CORES
    waves_f = wav_row[...].astype(F32)
    column = jnp.sum(jnp.where(across == natural, waves_f, 0.0), axis=1, keepdims=True)
    row = jnp.sum(jnp.where(across == place, column, 0.0), axis=0, keepdims=True)
    even = row - 2.0 * jnp.floor(row * 0.5) == 0.0
    parity = jnp.where(even, 1.0, -1.0)
    wcol[...] = jnp.broadcast_to(column, wcol.shape)

    chunk = waves // 4

    def table_part(step, carry):
        lat = step // 4
        begin = pl.multiple_of((step % 4) * chunk, chunk)
        count = jnp.full((chunk, LANES), counts_s[lat].astype(F32), F32)
        per_count = 1.0 / count
        waves_here = wcol[pl.ds(begin, chunk)]
        offset = iota((chunk, LANES), 1).astype(F32)
        c, s = turn(waves_here * offset, count, per_count)
        step_c, step_s = turn(waves_here * float(LANES), count, per_count)
        for a in range(points // LANES):
            at = slice(a * LANES, (a + 1) * LANES)
            table[lat, pl.ds(begin, chunk), at] = c.astype(BF16)
            table[lat, pl.ds(waves + begin, chunk), at] = s.astype(BF16)
            c, s = c * step_c - s * step_s, s * step_c + c * step_s
        return carry

    lax.fori_loop(0, LATS * 4, table_part, 0)

    arrived(0, s1_in)
    stage[...] = s1_in[...].astype(F32).reshape(stage.shape)
    slots = 4 * XS
    first_half = iota((zs, LANES), 1) < HALF
    for k in range(ds):
        for t in range(2):
            s2_out[k, t] = stage[pl.ds(2 * k + t, zs, stride=slots)].astype(BF16)
    send(1, lambda slot: s2_out.at[slot], s2_in, d, d_peers)

    degree = iota((1, trunc), 1).astype(F32)
    growth = degree * (degree + 1.0) / float(trunc * trunc)
    at_mode = iota((levels_all, LANES), 0)
    rates = jnp.zeros((levels_all, LANES), F32)
    for k in range(levels_all):
        rates = jnp.where(at_mode == k, rates_s[k], rates)
    inv[...] = 1.0 / (1.0 + rates[:, 0:1] * growth)

    r = iota((LANES, LANES), 0)
    field = (r // LEVS) % 4
    wanted = (r // HALF) * HALF + (r % LEVS) * 6 + 2 * field + (r // 32) % 2
    pick = jnp.where((iota((LANES, LANES), 1) == wanted) & (field < 3), 1.0, 0.0).astype(BF16)

    arrived(1, s2_in)

    def grid_pair(t, carry):
        got = s2_in[:, t].reshape(waves, LANES)
        coeffs = dot_rows(pick, got)
        blocks = []
        for low in range(2):
            lat = 2 * t + low
            cosine = coeffs[low * HALF : low * HALF + 24]
            sine = coeffs[low * HALF + 32 : low * HALF + 56]
            turned = parity * cosine
            turned_sine = parity * sine
            w = jnp.concatenate(
                [
                    jnp.concatenate([cosine, sine], 1),
                    jnp.concatenate([cosine, -sine], 1),
                    jnp.concatenate([turned, turned_sine], 1),
                    jnp.concatenate([turned, -turned_sine], 1),
                ],
                0,
            ).astype(BF16)
            grid = dot(w, table[lat]) * (1.0 / math.sqrt(2 * waves))
            count = counts_s[lat]
            quarter = count // 4
            j = iota((1, points), 1)
            share = jnp.where((j == 0) | (j == quarter), 0.5, 1.0)
            share = jnp.where(j > quarter, 0.0, share)
            tend = []
            for q in range(4):
                g = [grid[q * 24 + f * 8 : q * 24 + f * 8 + 8] for f in range(FIELDS)]
                tend.append([g[0] - g[1] * g[2], g[1] + g[0] * g[2], g[2] - g[0] * g[1]])
            folded = [[], [], [], []]
            for f in range(FIELDS):
                t0, t1, t2, t3 = (tend[q][f] * share for q in range(4))
                plus, minus = t0 + t1, t0 - t1
                plus_far, minus_far = t2 + t3, t2 - t3
                folded[0].append(plus + plus_far)
                folded[1].append(plus - plus_far)
                folded[2].append(minus + minus_far)
                folded[3].append(minus - minus_far)
            u = jnp.concatenate(folded[0] + folded[1] + folded[2] + folded[3], 0).astype(BF16)
            back = dot_rows(u, table[lat])
            count_f = jnp.full((1, waves), count.astype(F32), F32)
            factor = jnp.full((1, waves), weights_s[lat], F32) / jnp.sqrt(count_f)
            cos_out = jnp.where(even, back[0:24, :waves], back[24:48, :waves]) * factor
            sin_out = jnp.where(even, back[48:72, waves:], back[72:96, waves:]) * -factor
            for f in range(FIELDS):
                blocks.append(cos_out[f * 8 : f * 8 + 8])
                blocks.append(sin_out[f * 8 : f * 8 + 8])
            blocks.append(jnp.zeros((16, waves), F32))
        returned = jnp.concatenate(blocks, 0).astype(BF16)
        b2_out[:, t] = dot_rows(unit(waves), returned).astype(BF16).reshape(ds, zs, LANES)
        return carry

    lax.fori_loop(0, 2, grid_pair, 0)
    send(2, lambda slot: b2_out.at[slot], b2_in, d, d_peers)

    target = iota((1, lat_all), 1)
    spot = ((target // 8) % zs) * slots + (target // part_rows) * 4 + (target // 2) % 4
    line = iota((lat_all // 2, lat_all), 0)
    for low in range(2):
        pick_rows = jnp.where((spot == line) & (target % 2 == low), 1.0, 0.0).astype(BF16)
        lp[low] = dot(pick_rows, leg[...]).astype(BF16)

    arrived(2, b2_in)
    stage[...] = b2_in[...].astype(F32).reshape(stage.shape)
    for to in range(zs):
        b1_out[to] = stage[pl.ds(to, slots, stride=zs)].astype(BF16)
    send(3, lambda slot: b1_out.at[slot], b1_in, z, z_peers)

    arrived(5, v_in)
    lane = iota((levels_all, 4 * levels_all), 1)
    whole = v_in[0]
    for k in range(1, ys):
        whole = whole + v_in[k]
    whole_high = whole.astype(BF16).astype(F32)
    into = jnp.where(lane < 2 * levels_all, whole_high, whole - whole_high).astype(BF16)
    lane = iota((LEVS, 4 * levels_all), 1)
    whole = jnp.zeros((LEVS, 4 * levels_all), F32)
    for k in range(levels_all):
        whole = jnp.where(lane % levels_all == k, vout_ref[:, k : k + 1], whole)
    whole_high = whole.astype(BF16).astype(F32)
    onto = jnp.where(lane < 2 * levels_all, whole_high, whole - whole_high).astype(BF16)

    def place_rows(begin, value):
        for a in range(trunc // LANES):
            out32[a, pl.ds(begin, LEVS, stride=6)] = value[:, a * LANES : (a + 1) * LANES]

    def high_low(value):
        high = value.astype(BF16)
        low = (value - high.astype(F32)).astype(BF16)
        return jnp.concatenate([high, low, high, low], 0)

    arrived(3, b1_in)
    back = dot_rows(unit(LANES), b1_in[...].reshape(lat_all // 2, LANES)).astype(BF16)
    y_out[0] = back[0:16]
    y_out[1] = back[HALF : HALF + 16]
    send(4, lambda slot: y_out, y_in, y, y_peers)
    others = dot(back[16:48], lp[0]) + dot(back[HALF + 16 : HALF + 48], lp[1])
    others = jnp.where(kept, others, 0.0)
    for f in (1, 2):
        for part in range(2):
            begin = (f - 1) * 16 + part * 8
            place_rows(2 * f + part, others[begin : begin + LEVS])

    arrived(4, y_in)
    first = y_in[:, 0].reshape(ys * 16, lat_all // 2)
    second = y_in[:, 1].reshape(ys * 16, lat_all // 2)
    diverg = dot(first, lp[0]) + dot(second, lp[1])
    diverg = jnp.where(kept, diverg, 0.0)
    for part in range(2):
        of_part = [diverg[k * 16 + part * 8 : k * 16 + part * 8 + 8] for k in range(ys)]
        modes = dot(into, high_low(jnp.concatenate(of_part, 0)))
        solved = dot(onto, high_low(modes * inv[...]))
        place_rows(part, solved)
    for a in range(trunc // LANES):
        out_ref[0, :, a * LANES : (a + 1) * LANES] = out32[a].astype(BF16)

    sent(0, s1_in, zs - 1)
    sent(1, s2_in, ds - 1)
    sent(2, b2_in, ds - 1)
    sent(3, b1_in, zs - 1)
    sent(4, y_in, ys - 1)
    sent(5, v_in, ys - 1)


def body(spec_in, legendre, wavenum, counts, quad_weights, vert_in, vert_out, mode_rates, zs, ys):
    _, columns, trunc = spec_in.shape
    ds = XS * CORES
    waves = ds * zs
    lat_all = waves * LATS
    levels_all = ys * LEVS
    points = -(-(PTS // 4 + 1) // LANES) * LANES
    vmem = pl.BlockSpec(memory_space=pltpu.VMEM)
    smem = pl.BlockSpec(memory_space=pltpu.SMEM)
    by_z = (zs, 4 * XS, LANES)
    by_d = (ds, 2, zs, LANES)
    return pl.pallas_call(
        functools.partial(kernel, zs, ys),
        out_shape=jax.ShapeDtypeStruct((1, columns, trunc), BF16),
        in_specs=[vmem, pl.BlockSpec(memory_space=pl.ANY), vmem, smem, smem, smem, smem, vmem, vmem],
        out_specs=vmem,
        scratch_shapes=[
            pltpu.VMEM((lat_all, trunc), BF16),
            pltpu.VMEM((LANES, trunc), BF16),
            pltpu.VMEM((lat_all, LANES), F32),
            pltpu.VMEM((lat_all // 2, LANES), F32),
            pltpu.VMEM((waves, LANES), F32),
            pltpu.VMEM((LATS, 2 * waves, points), BF16),
            pltpu.VMEM((2, lat_all // 2, trunc), BF16),
            pltpu.VMEM((levels_all, trunc), F32),
            pltpu.VMEM((trunc // LANES, columns, LANES), F32),
            pltpu.VMEM(by_z, BF16),
            pltpu.VMEM(by_z, BF16),
            pltpu.VMEM(by_d, BF16),
            pltpu.VMEM(by_d, BF16),
            pltpu.VMEM(by_d, BF16),
            pltpu.VMEM(by_d, BF16),
            pltpu.VMEM(by_z, BF16),
            pltpu.VMEM(by_z, BF16),
            pltpu.VMEM((2, 16, lat_all // 2), BF16),
            pltpu.VMEM((ys, 2, 16, lat_all // 2), BF16),
            pltpu.VMEM((levels_all, 4 * levels_all), F32),
            pltpu.VMEM((ys, levels_all, 4 * levels_all), F32),
            pltpu.SemaphoreType.DMA((XS,)),
            pltpu.SemaphoreType.DMA((6,)),
            pltpu.SemaphoreType.DMA((6,)),
        ],
        compiler_params=pltpu.CompilerParams(
            collective_id=0, has_side_effects=True, vmem_limit_bytes=48 * 1024 * 1024
        ),
    )(
        spec_in, legendre, wavenum.reshape(1, -1), wavenum, counts, quad_weights, mode_rates,
        vert_in, vert_out,
    )


def solution(mesh):
    zs = mesh.shape["lat"] // (XS * CORES)
    return jax.shard_map(
        functools.partial(body, zs=zs, ys=mesh.shape["lev"]),
        mesh=mesh,
        in_specs=(
            P("lat", "lev", None),
            P("lat", None, None),
            P(),
            P("lat"),
            P("lat"),
            P(None, "lev"),
            P("lev", None),
            P(),
        ),
        out_specs=P("lat", "lev", None),
        check_vma=False,
    )
```

```python
import functools
import math

import jax
import jax.numpy as jnp
from jax import lax
from jax.experimental import pallas as pl
from jax.experimental.pallas import tpu as pltpu
from jax.sharding import PartitionSpec as P

PTS = 5136
FIELDS = 3
XS = 4
CORES = 2
LATS = 4
LEVS = 8
LANES = 128
HALF = 64

F32 = jnp.float32
BF16 = jnp.bfloat16
MESH = pl.DeviceIdType.MESH

ROWS_BY_ROWS = (((1,), (1,)), ((), ()))


def dot(a, b):
    return jnp.dot(a, b, preferred_element_type=F32)


def dot_rows(a, b):
    return lax.dot_general(a, b, ROWS_BY_ROWS, preferred_element_type=F32)


def iota(shape, dim):
    return lax.broadcasted_iota(jnp.int32, shape, dim)


def unit(size):
    return jnp.where(iota((size, size), 0) == iota((size, size), 1), 1.0, 0.0).astype(BF16)


def half_up(value):
    return jnp.floor(value + 0.5)


def turn(steps, count, per_count):
    left = steps - half_up(steps * per_count) * count
    x = left * per_count * math.pi
    y = x * x
    s = -1.0 / 39916800
    for term in (1.0 / 362880, -1.0 / 5040, 1.0 / 120, -1.0 / 6, 1.0):
        s = s * y + term
    s = s * x
    c = 1.0 / 479001600
    for term in (-1.0 / 3628800, 1.0 / 40320, -1.0 / 720, 1.0 / 24, -0.5, 1.0):
        c = c * y + term
    return 1.0 - 2.0 * s * s, 2.0 * s * c


def kernel(
    zs, ys, spec_hbm, leg_hbm, wav_hbm, wav_row_hbm, counts_hbm, weights_hbm, rates_hbm, vin_hbm, vout_hbm,
    out_ref,
    spec_ref, wav_row, vin_ref, vout_ref, wav_s, counts_s, weights_s, rates_s,
    leg, spec2, fou, stage, wcol, table, lp, inv, out32,
    s1_out, s1_in, s2_out, s2_in, b_out, b_in, y_out, y_in, v_out, v_in,
    load_sem, leg_sem, send_sem, recv_sem,
):
    ds = XS * CORES
    waves = ds * zs
    lat_all = waves * LATS
    trunc = spec_ref.shape[1]
    points = table.shape[2]
    levels_all = ys * LEVS
    me = lax.axis_index("lat")
    y = lax.axis_index("lev")
    x = me // (zs * CORES)
    z = (me // CORES) % zs
    core = me % CORES
    d = x * CORES + core

    def device(to_x, to_z, to_core):
        return (to_x * (zs * CORES) + to_z * CORES + to_core, y)

    z_peers = []
    for i in range(zs - 1):
        away = zs // 2 - (i + 1) // 2 if i % 2 else zs // 2 + i // 2
        to = (z + away) % zs
        z_peers.append((to, device(x, to, core)))
    d_away = [(k, c) for k in sorted(range(XS), key=lambda k: -min(k, XS - k)) for c in range(CORES)]
    d_peers = []
    for k, c in d_away:
        to_x, to_core = (x + k) % XS, (core + c) % CORES
        if (k, c) != (0, 0):
            d_peers.append((to_x * CORES + to_core, device(to_x, z, to_core)))
    y_peers = []
    for k in range(1, ys):
        to = (y + k) % ys
        y_peers.append((to, (me, to)))

    barrier = pltpu.get_barrier_semaphore()
    for _, to in z_peers + d_peers + y_peers:
        pl.semaphore_signal(barrier, inc=1, device_id=to, device_id_type=MESH)

    loads = []
    for source, target in (
        (spec_hbm.at[0], spec_ref), (wav_hbm, wav_s), (counts_hbm, counts_s), (weights_hbm, weights_s),
        (rates_hbm, rates_s), (wav_row_hbm, wav_row), (vin_hbm, vin_ref), (vout_hbm, vout_ref),
    ):
        loads.append(pltpu.make_async_copy(source, target, load_sem.at[len(loads)]))
        loads[-1].start()
    part_rows = lat_all // XS
    leg_loads = []
    for k in range(XS):
        rows = pl.ds(k * part_rows, part_rows)
        leg_loads.append(pltpu.make_async_copy(leg_hbm.at[0, rows], leg.at[rows], leg_sem.at[k]))
        leg_loads[-1].start()

    def send(number, source, arrive, slot, peers):
        pltpu.make_async_copy(source(slot), arrive.at[slot], recv_sem.at[number]).start()
        for to, to_device in peers:
            pltpu.make_async_remote_copy(
                src_ref=source(to), dst_ref=arrive.at[slot],
                send_sem=send_sem.at[number], recv_sem=recv_sem.at[number],
                device_id=to_device, device_id_type=MESH,
            ).start()

    def arrived(number, arrive):
        pltpu.make_async_copy(arrive, arrive, recv_sem.at[number]).wait()

    def sent(number, arrive, count):
        part = arrive.at[pl.ds(0, count)]
        pltpu.make_async_copy(part, part, send_sem.at[number]).wait()

    loads[0].wait()
    loads[1].wait()
    order = wav_s[me]
    kept = iota((1, trunc), 1) >= order
    columns = spec_ref.shape[0]
    masked = jnp.where(kept, spec_ref[...].astype(F32), 0.0).astype(BF16)
    blank = jnp.zeros((HALF - columns, trunc), BF16)
    spec2[0:columns] = masked
    spec2[columns:HALF] = blank
    spec2[HALF : HALF + columns] = masked
    spec2[HALF + columns :] = blank

    for k in range(XS):
        leg_loads[k].wait()
        rows = pl.ds(k * part_rows, part_rows)
        fou[rows] = dot_rows(leg[rows], spec2[...])

    first_half = iota((LATS, LANES), 1) < HALF
    for to in range(zs):
        for k in range(XS):
            low = fou[pl.ds(k * part_rows + 8 * to, 4, stride=2)]
            high = fou[pl.ds(k * part_rows + 8 * to + 1, 4, stride=2)]
            stage[pl.ds(to * 4 * XS + 4 * k, 4)] = jnp.where(first_half, low, high)
    s1_out[...] = stage[...].astype(BF16).reshape(s1_out.shape)

    pl.semaphore_wait(barrier, len(z_peers) + len(d_peers) + len(y_peers))
    send(0, lambda slot: s1_out.at[slot], s1_in, z, z_peers)

    for load in loads[2:]:
        load.wait()

    v_out[...] = jnp.zeros(v_out.shape, F32)
    v_out[:, 0:levels_all] = vin_ref[...]
    send(4, lambda slot: v_out, v_in, y, y_peers)

    place = iota((waves, waves), 0)
    across = iota((waves, waves), 1)
    natural = (place // (CORES * zs)) * (CORES * zs) + (place % zs) * CORES + (place // zs) % CORES
    waves_f = wav_row[...].astype(F32)
    column = jnp.sum(jnp.where(across == natural, waves_f, 0.0), axis=1, keepdims=True)
    row = jnp.sum(jnp.where(across == place, column, 0.0), axis=0, keepdims=True)
    even = row - 2.0 * jnp.floor(row * 0.5) == 0.0
    parity = jnp.where(even, 1.0, -1.0)
    wcol[...] = jnp.broadcast_to(column, wcol.shape)

    chunk = waves // 4

    def table_part(step, carry):
        lat = step // 4
        begin = pl.multiple_of((step % 4) * chunk, chunk)
        count = jnp.full((chunk, LANES), counts_s[lat].astype(F32), F32)
        per_count = 1.0 / count
        waves_here = wcol[pl.ds(begin, chunk)]
        offset = iota((chunk, LANES), 1).astype(F32)
        c, s = turn(waves_here * offset, count, per_count)
        step_c, step_s = turn(waves_here * float(LANES), count, per_count)
        for a in range(points // LANES):
            at = slice(a * LANES, (a + 1) * LANES)
            table[lat, pl.ds(begin, chunk), at] = c.astype(BF16)
            table[lat, pl.ds(waves + begin, chunk), at] = s.astype(BF16)
            c, s = c * step_c - s * step_s, s * step_c + c * step_s
        return carry

    lax.fori_loop(0, LATS * 4, table_part, 0)

    arrived(0, s1_in)
    stage[...] = s1_in[...].astype(F32).reshape(stage.shape)
    slots = 4 * XS
    first_half = iota((zs, LANES), 1) < HALF
    for k in range(ds):
        for t in range(2):
            s2_out[k, t] = stage[pl.ds(2 * k + t, zs, stride=slots)].astype(BF16)
    send(1, lambda slot: s2_out.at[slot], s2_in, d, d_peers)

    r = iota((LANES, LANES), 0)
    field = (r // LEVS) % 4
    wanted = (r // HALF) * HALF + (r % LEVS) * 6 + 2 * field + (r // 32) % 2
    pick = jnp.where((iota((LANES, LANES), 1) == wanted) & (field < 3), 1.0, 0.0).astype(BF16)

    arrived(1, s2_in)

    def grid_pair(t):
        got = s2_in[:, t].reshape(waves, LANES)
        coeffs = dot_rows(pick, got)
        blocks = []
        for low in range(2):
            lat = 2 * t + low
            cosine = coeffs[low * HALF : low * HALF + 24]
            sine = coeffs[low * HALF + 32 : low * HALF + 56]
            turned = parity * cosine
            turned_sine = parity * sine
            w = jnp.concatenate(
                [
                    jnp.concatenate([cosine, sine], 1),
                    jnp.concatenate([cosine, -sine], 1),
                    jnp.concatenate([turned, turned_sine], 1),
                    jnp.concatenate([turned, -turned_sine], 1),
                ],
                0,
            ).astype(BF16)
            grid = dot(w, table[lat]) * (1.0 / math.sqrt(2 * waves))
            count = counts_s[lat]
            quarter = count // 4
            j = iota((1, points), 1)
            share = jnp.where((j == 0) | (j == quarter), 0.5, 1.0)
            share = jnp.where(j > quarter, 0.0, share)
            tend = []
            for q in range(4):
                g = [grid[q * 24 + f * 8 : q * 24 + f * 8 + 8] for f in range(FIELDS)]
                tend.append([g[0] - g[1] * g[2], g[1] + g[0] * g[2], g[2] - g[0] * g[1]])
            folded = [[], [], [], []]
            for f in range(FIELDS):
                t0, t1, t2, t3 = (tend[q][f] * share for q in range(4))
                plus, minus = t0 + t1, t0 - t1
                plus_far, minus_far = t2 + t3, t2 - t3
                folded[0].append(plus + plus_far)
                folded[1].append(plus - plus_far)
                folded[2].append(minus + minus_far)
                folded[3].append(minus - minus_far)
            u = jnp.concatenate(folded[0] + folded[1] + folded[2] + folded[3], 0).astype(BF16)
            back = dot_rows(u, table[lat])
            count_f = jnp.full((1, waves), count.astype(F32), F32)
            factor = jnp.full((1, waves), weights_s[lat], F32) / jnp.sqrt(count_f)
            cos_out = jnp.where(even, back[0:24, :waves], back[24:48, :waves]) * factor
            sin_out = jnp.where(even, back[48:72, waves:], back[72:96, waves:]) * -factor
            for f in range(FIELDS):
                blocks.append(cos_out[f * 8 : f * 8 + 8])
                blocks.append(sin_out[f * 8 : f * 8 + 8])
            blocks.append(jnp.zeros((16, waves), F32))
        returned = jnp.concatenate(blocks, 0).astype(BF16)
        stage[pl.ds(t, waves, stride=2)] = dot_rows(unit(waves), returned)

    for t in range(2):
        grid_pair(t)
    b_out[...] = stage[...].astype(BF16).reshape(b_out.shape)
    def send_back(away, pairs):
        to_z = (z + away) % zs
        for k, c in pairs:
            to_x, to_core = (x + k) % XS, (core + c) % CORES
            pltpu.make_async_remote_copy(
                src_ref=b_out.at[(to_x * CORES + to_core) * zs + to_z], dst_ref=b_in.at[me],
                send_sem=send_sem.at[2], recv_sem=recv_sem.at[2],
                device_id=device(to_x, to_z, to_core), device_id_type=MESH,
            ).start()

    def send_ring(i, carry):
        odd = i % 2
        send_back(odd * (zs // 2 - (i + 1) // 2) + (1 - odd) * (zs // 2 + i // 2), d_away)
        return carry

    lax.fori_loop(0, zs - 1, send_ring, 0)
    send_back(0, [pair for pair in d_away if pair != (0, 0)])
    pltpu.make_async_copy(b_out.at[d * zs + z], b_in.at[me], recv_sem.at[2]).start()

    target = iota((1, lat_all), 1)
    line = iota((lat_all // 2, lat_all), 0)
    for low in range(2):
        pick_rows = jnp.where(target == 2 * line + low, 1.0, 0.0).astype(BF16)
        lp[low] = dot(pick_rows, leg[...]).astype(BF16)

    degree = iota((1, trunc), 1).astype(F32)
    growth = degree * (degree + 1.0) / float(trunc * trunc)
    at_mode = iota((levels_all, LANES), 0)
    rates = jnp.zeros((levels_all, LANES), F32)
    for k in range(levels_all):
        rates = jnp.where(at_mode == k, rates_s[k], rates)
    inv[...] = 1.0 / (1.0 + rates[:, 0:1] * growth)

    arrived(4, v_in)
    whole = v_in[...].reshape(levels_all, LANES)
    whole_high = whole.astype(BF16).astype(F32)
    whole_low = whole - whole_high
    into = jnp.concatenate([whole_high, whole_high, whole_low, whole_low], 0).astype(BF16)
    into = dot_rows(unit(LANES), into)[0:levels_all].astype(BF16)
    lane = iota((LEVS, 4 * levels_all), 1)
    whole = jnp.zeros((LEVS, 4 * levels_all), F32)
    for k in range(levels_all):
        whole = jnp.where(lane % levels_all == k, vout_ref[:, k : k + 1], whole)
    whole_high = whole.astype(BF16).astype(F32)
    onto = jnp.where(lane < 2 * levels_all, whole_high, whole - whole_high).astype(BF16)

    def place_rows(begin, value):
        for a in range(trunc // LANES):
            out32[a, pl.ds(begin, LEVS, stride=6)] = value[:, a * LANES : (a + 1) * LANES]

    def high_low(value):
        high = value.astype(BF16)
        low = (value - high.astype(F32)).astype(BF16)
        return jnp.concatenate([high, low, high, low], 0)

    arrived(2, b_in)
    back = dot_rows(unit(LANES), b_in[...].reshape(lat_all // 2, LANES)).astype(BF16)
    y_out[0] = back[0:16]
    y_out[1] = back[HALF : HALF + 16]
    send(3, lambda slot: y_out, y_in, y, y_peers)
    others = dot(back[16:48], lp[0]) + dot(back[HALF + 16 : HALF + 48], lp[1])
    others = jnp.where(kept, others, 0.0)
    for f in (1, 2):
        for part in range(2):
            begin = (f - 1) * 16 + part * 8
            place_rows(2 * f + part, others[begin : begin + LEVS])

    arrived(3, y_in)
    first = y_in[:, 0].reshape(ys * 16, lat_all // 2)
    second = y_in[:, 1].reshape(ys * 16, lat_all // 2)
    diverg = dot(first, lp[0]) + dot(second, lp[1])
    diverg = jnp.where(kept, diverg, 0.0)
    for part in range(2):
        of_part = [diverg[k * 16 + part * 8 : k * 16 + part * 8 + 8] for k in range(ys)]
        modes = dot(into, high_low(jnp.concatenate(of_part, 0)))
        solved = dot(onto, high_low(modes * inv[...]))
        place_rows(part, solved)
    for a in range(trunc // LANES):
        out_ref[0, :, a * LANES : (a + 1) * LANES] = out32[a].astype(BF16)

    sent(0, s1_in, zs - 1)
    sent(1, s2_in, ds - 1)
    sent(2, b_in, waves - 1)
    sent(3, y_in, ys - 1)
    sent(4, v_in, ys - 1)


def body(spec_in, legendre, wavenum, counts, quad_weights, vert_in, vert_out, mode_rates, zs, ys):
    _, columns, trunc = spec_in.shape
    ds = XS * CORES
    waves = ds * zs
    lat_all = waves * LATS
    levels_all = ys * LEVS
    points = -(-(PTS // 4 + 1) // LANES) * LANES
    any_place = pl.BlockSpec(memory_space=pl.ANY)
    by_z = (zs, 4 * XS, LANES)
    by_d = (ds, 2, zs, LANES)
    return pl.pallas_call(
        functools.partial(kernel, zs, ys),
        out_shape=jax.ShapeDtypeStruct((1, columns, trunc), BF16),
        in_specs=[any_place] * 9,
        out_specs=pl.BlockSpec(memory_space=pltpu.VMEM),
        scratch_shapes=[
            pltpu.VMEM((columns, trunc), BF16),
            pltpu.VMEM((1, waves), jnp.int32),
            pltpu.VMEM((LEVS, levels_all), F32),
            pltpu.VMEM((LEVS, levels_all), F32),
            pltpu.SMEM((waves,), jnp.int32),
            pltpu.SMEM((LATS,), jnp.int32),
            pltpu.SMEM((LATS,), F32),
            pltpu.SMEM((levels_all,), F32),
            pltpu.VMEM((lat_all, trunc), BF16),
            pltpu.VMEM((LANES, trunc), BF16),
            pltpu.VMEM((lat_all, LANES), F32),
            pltpu.VMEM((lat_all // 2, LANES), F32),
            pltpu.VMEM((waves, LANES), F32),
            pltpu.VMEM((LATS, 2 * waves, points), BF16),
            pltpu.VMEM((2, lat_all // 2, trunc), BF16),
            pltpu.VMEM((levels_all, trunc), F32),
            pltpu.VMEM((trunc // LANES, columns, LANES), F32),
            pltpu.VMEM(by_z, BF16),
            pltpu.VMEM(by_z, BF16),
            pltpu.VMEM(by_d, BF16),
            pltpu.VMEM(by_d, BF16),
            pltpu.VMEM((waves, 2, LANES), BF16),
            pltpu.VMEM((waves, 2, LANES), BF16),
            pltpu.VMEM((2, 16, lat_all // 2), BF16),
            pltpu.VMEM((ys, 2, 16, lat_all // 2), BF16),
            pltpu.VMEM((LEVS, LANES), F32),
            pltpu.VMEM((ys, LEVS, LANES), F32),
            pltpu.SemaphoreType.DMA((8,)),
            pltpu.SemaphoreType.DMA((XS,)),
            pltpu.SemaphoreType.DMA((5,)),
            pltpu.SemaphoreType.DMA((5,)),
        ],
        compiler_params=pltpu.CompilerParams(
            collective_id=0, has_side_effects=True, vmem_limit_bytes=60 * 1024 * 1024
        ),
    )(
        spec_in, legendre, wavenum, wavenum.reshape(1, -1), counts, quad_weights, mode_rates,
        vert_in.T, vert_out,
    )


def solution(mesh):
    zs = mesh.shape["lat"] // (XS * CORES)
    return jax.shard_map(
        functools.partial(body, zs=zs, ys=mesh.shape["lev"]),
        mesh=mesh,
        in_specs=(
            P("lat", "lev", None),
            P("lat", None, None),
            P(),
            P("lat"),
            P("lat"),
            P(None, "lev"),
            P("lev", None),
            P(),
        ),
        out_specs=P("lat", "lev", None),
        check_vma=False,
    )
```

```python
import functools
import math

import jax
import jax.numpy as jnp
from jax import lax
from jax.experimental import pallas as pl
from jax.experimental.pallas import tpu as pltpu
from jax.sharding import PartitionSpec as P

PTS = 5136
FIELDS = 3
XS = 4
CORES = 2
LATS = 4
LEVS = 8
LANES = 128
HALF = 64

F32 = jnp.float32
BF16 = jnp.bfloat16
MESH = pl.DeviceIdType.MESH

ROWS_BY_ROWS = (((1,), (1,)), ((), ()))


def dot(a, b):
    return jnp.dot(a, b, preferred_element_type=F32)


def dot_rows(a, b):
    return lax.dot_general(a, b, ROWS_BY_ROWS, preferred_element_type=F32)


def iota(shape, dim):
    return lax.broadcasted_iota(jnp.int32, shape, dim)


def unit(size):
    return jnp.where(iota((size, size), 0) == iota((size, size), 1), 1.0, 0.0).astype(BF16)


def half_up(value):
    return jnp.floor(value + 0.5)


def turn(steps, count, per_count):
    left = steps - half_up(steps * per_count) * count
    x = left * per_count * math.pi
    y = x * x
    s = -1.0 / 39916800
    for term in (1.0 / 362880, -1.0 / 5040, 1.0 / 120, -1.0 / 6, 1.0):
        s = s * y + term
    s = s * x
    c = 1.0 / 479001600
    for term in (-1.0 / 3628800, 1.0 / 40320, -1.0 / 720, 1.0 / 24, -0.5, 1.0):
        c = c * y + term
    return 1.0 - 2.0 * s * s, 2.0 * s * c


def kernel(
    zs, ys, spec_hbm, leg_hbm, wav_hbm, wav_row_hbm, counts_hbm, weights_hbm, rates_hbm, vin_hbm, vout_hbm,
    out_ref,
    spec_ref, wav_row, vin_ref, vout_ref, wav_s, counts_s, weights_s, rates_s,
    leg, spec2, fou, stage, stage_back, wcol, table, table_back, lp, inv, out32,
    a_out, a_in, b_out, b_in, y_out, y_in, v_out, v_in,
    load_sem, leg_sem, send_sem, recv_sem, all_in,
):
    ds = XS * CORES
    waves = ds * zs
    lat_all = waves * LATS
    trunc = spec_ref.shape[1]
    points = table.shape[2]
    levels_all = ys * LEVS
    me = lax.axis_index("lat")
    y = lax.axis_index("lev")
    x = me // (zs * CORES)
    z = (me // CORES) % zs
    core = me % CORES
    d = x * CORES + core

    def device(to_x, to_z, to_core):
        return (to_x * (zs * CORES) + to_z * CORES + to_core, y)

    def ring_away(i):
        odd = i % 2
        return odd * (zs // 2 - (i + 1) // 2) + (1 - odd) * (zs // 2 + i // 2)

    z_peers = []
    for i in range(zs - 1):
        to = (z + ring_away(i)) % zs
        z_peers.append((to, device(x, to, core)))
    d_away = [(k, c) for k in sorted(range(XS), key=lambda k: -min(k, XS - k)) for c in range(CORES)]
    d_peers = []
    for k, c in d_away:
        to_x, to_core = (x + k) % XS, (core + c) % CORES
        if (k, c) != (0, 0):
            d_peers.append((to_x * CORES + to_core, device(to_x, z, to_core)))
    y_peers = []
    for k in sorted(range(1, ys), key=lambda k: -min(k, ys - k)):
        to = (y + k) % ys
        y_peers.append((to, (me, to)))

    barrier = pltpu.get_barrier_semaphore()
    for _, to in z_peers + d_peers + y_peers:
        pl.semaphore_signal(barrier, inc=1, device_id=to, device_id_type=MESH)

    loads = []
    for source, target in (
        (spec_hbm.at[0], spec_ref), (wav_hbm, wav_s), (counts_hbm, counts_s), (weights_hbm, weights_s),
        (rates_hbm, rates_s), (wav_row_hbm, wav_row), (vin_hbm, vin_ref), (vout_hbm, vout_ref),
    ):
        loads.append(pltpu.make_async_copy(source, target, load_sem.at[len(loads)]))
        loads[-1].start()
    part_rows = lat_all // XS
    leg_loads = []
    for k in range(XS):
        rows = pl.ds(k * part_rows, part_rows)
        leg_loads.append(pltpu.make_async_copy(leg_hbm.at[0, rows], leg.at[rows], leg_sem.at[k]))
        leg_loads[-1].start()

    def send(number, source, arrive, slot, peers):
        pltpu.make_async_copy(source(slot), arrive.at[slot], recv_sem.at[number]).start()
        for to, to_device in peers:
            pltpu.make_async_remote_copy(
                src_ref=source(to), dst_ref=arrive.at[slot],
                send_sem=send_sem.at[number], recv_sem=recv_sem.at[number],
                device_id=to_device, device_id_type=MESH,
            ).start()

    def arrived(number, arrive):
        pltpu.make_async_copy(arrive, arrive, recv_sem.at[number]).wait()

    def sent(number, arrive, count):
        part = arrive.at[pl.ds(0, count)]
        pltpu.make_async_copy(part, part, send_sem.at[number]).wait()

    loads[0].wait()
    loads[1].wait()
    order = wav_s[me]
    kept = iota((1, trunc), 1) >= order
    columns = spec_ref.shape[0]
    masked = jnp.where(kept, spec_ref[...].astype(F32), 0.0).astype(BF16)
    blank = jnp.zeros((HALF - columns, trunc), BF16)
    spec2[0:columns] = masked
    spec2[columns:HALF] = blank
    spec2[HALF : HALF + columns] = masked
    spec2[HALF + columns :] = blank

    for k in range(XS):
        leg_loads[k].wait()
        rows = pl.ds(k * part_rows, part_rows)
        fou[rows] = dot_rows(leg[rows], spec2[...])
    first_half = iota((lat_all // 2, LANES), 1) < HALF
    low = fou[pl.ds(0, lat_all // 2, stride=2)]
    high = fou[pl.ds(1, lat_all // 2, stride=2)]
    a_out[...] = jnp.where(first_half, low, high).astype(BF16).reshape(a_out.shape)

    def push(number, leave, arrive, to_x, to_z, to_core):
        to = device(to_x, to_z, to_core)
        pltpu.make_async_remote_copy(
            src_ref=leave.at[to[0]], dst_ref=arrive.at[me],
            send_sem=send_sem.at[number], recv_sem=recv_sem.at[number],
            device_id=to, device_id_type=MESH,
        ).start()

    def push_ring(number, leave, arrive, pairs, own):
        def push_pairs(away, some):
            for k, c in some:
                push(number, leave, arrive, (x + k) % XS, (z + away) % zs, (core + c) % CORES)

        def one(i, carry):
            push_pairs(ring_away(i), pairs)
            return carry

        lax.fori_loop(0, zs - 1, one, 0)
        push_pairs(0, own)

    others_here = [pair for pair in d_away if pair != (0, 0)]

    pl.semaphore_wait(barrier, len(z_peers) + len(d_peers) + len(y_peers))
    for _, to in d_peers:
        pl.semaphore_signal(all_in, inc=1, device_id=to, device_id_type=MESH)
    push_ring(0, a_out, a_in, [(0, 0)], [])
    pltpu.make_async_copy(a_out.at[me], a_in.at[me], recv_sem.at[0]).start()
    pl.semaphore_wait(all_in, len(d_peers))
    push_ring(0, a_out, a_in, others_here, others_here)

    for load in loads[2:]:
        load.wait()

    v_out[...] = jnp.zeros(v_out.shape, F32)
    v_out[:, 0:levels_all] = vin_ref[...]
    send(4, lambda slot: v_out, v_in, y, y_peers)

    place = iota((waves, waves), 0)
    across = iota((waves, waves), 1)
    row = wav_row[...].astype(F32)
    even = row - 2.0 * jnp.floor(row * 0.5) == 0.0
    parity = jnp.where(even, 1.0, -1.0)
    column = jnp.sum(jnp.where(across == place, row, 0.0), axis=1, keepdims=True)
    wcol[...] = jnp.broadcast_to(column, wcol.shape)

    def table_part(step, carry):
        lat = step // 4
        chunk = waves // 4
        begin = pl.multiple_of((step % 4) * chunk, chunk)
        count = jnp.full((chunk, LANES), counts_s[lat].astype(F32), F32)
        per_count = 1.0 / count
        waves_here = wcol[pl.ds(begin, chunk)]
        offset = iota((chunk, LANES), 1).astype(F32)
        c, s = turn(waves_here * offset, count, per_count)
        step_c, step_s = turn(waves_here * float(LANES), count, per_count)
        for a in range(points // LANES):
            at = slice(a * LANES, (a + 1) * LANES)
            table[lat, pl.ds(begin, chunk), at] = c.astype(BF16)
            table[lat, pl.ds(waves + begin, chunk), at] = s.astype(BF16)
            c, s = c * step_c - s * step_s, s * step_c + c * step_s
        return carry

    lax.fori_loop(0, LATS * 4, table_part, 0)

    def back_part(step, carry):
        lat = step // 4
        chunk = LANES // 4
        begin = pl.multiple_of((step % 4) * chunk, chunk)
        count = jnp.full((chunk, waves), counts_s[lat].astype(F32), F32)
        per_count = 1.0 / count
        quarter = counts_s[lat] // 4
        offset = (iota((chunk, waves), 0) + begin).astype(F32)
        c, s = turn(row * offset, count, per_count)
        step_c, step_s = turn(jnp.broadcast_to(row * float(LANES), (chunk, waves)), count, per_count)
        for a in range(points // LANES):
            at = pl.ds(a * LANES + begin, chunk)
            j = iota((chunk, waves), 0) + (a * LANES + begin)
            share = jnp.where((j == 0) | (j == quarter), 0.5, jnp.where(j > quarter, 0.0, 1.0))
            table_back[lat, at, 0:waves] = (c * share).astype(BF16)
            table_back[lat, at, waves:] = (s * share).astype(BF16)
            c, s = c * step_c - s * step_s, s * step_c + c * step_s
        return carry

    lax.fori_loop(0, LATS * 4, back_part, 0)

    r = iota((LANES, LANES), 0)
    field = (r // LEVS) % 4
    wanted = (r // HALF) * HALF + (r % LEVS) * 6 + 2 * field + (r // 32) % 2
    pick = jnp.where((iota((LANES, LANES), 1) == wanted) & (field < 3), 1.0, 0.0).astype(BF16)


    def grid_pair(t):
        got = stage[pl.ds(t, waves, stride=2)].astype(BF16)
        coeffs = dot_rows(pick, got) * (1.0 / math.sqrt(2 * waves))
        blocks = []
        for low in range(2):
            lat = 2 * t + low
            cosine = coeffs[low * HALF : low * HALF + 24]
            sine = coeffs[low * HALF + 32 : low * HALF + 56]
            turned = parity * cosine
            turned_sine = parity * sine
            w = jnp.concatenate(
                [
                    jnp.concatenate([cosine, sine], 1),
                    jnp.concatenate([cosine, -sine], 1),
                    jnp.concatenate([turned, turned_sine], 1),
                    jnp.concatenate([turned, -turned_sine], 1),
                ],
                0,
            ).astype(BF16)
            grid = dot(w, table[lat])
            count = counts_s[lat]
            tend = []
            for q in range(4):
                g = [grid[q * 24 + f * 8 : q * 24 + f * 8 + 8] for f in range(FIELDS)]
                tend.append([g[0] - g[1] * g[2], g[1] + g[0] * g[2], g[2] - g[0] * g[1]])
            folded = [[], [], [], []]
            for f in range(FIELDS):
                t0, t1, t2, t3 = (tend[q][f] for q in range(4))
                plus, minus = t0 + t1, t0 - t1
                plus_far, minus_far = t2 + t3, t2 - t3
                folded[0].append(plus + plus_far)
                folded[1].append(plus - plus_far)
                folded[2].append(minus + minus_far)
                folded[3].append(minus - minus_far)
            u = jnp.concatenate(folded[0] + folded[1] + folded[2] + folded[3], 0).astype(BF16)
            back = dot(u, table_back[lat])
            count_f = jnp.full((1, waves), count.astype(F32), F32)
            factor = jnp.full((1, waves), weights_s[lat], F32) / jnp.sqrt(count_f)
            cos_out = jnp.where(even, back[0:24, :waves], back[24:48, :waves]) * factor
            sin_out = jnp.where(even, back[48:72, waves:], back[72:96, waves:]) * -factor
            for f in range(FIELDS):
                blocks.append(cos_out[f * 8 : f * 8 + 8])
                blocks.append(sin_out[f * 8 : f * 8 + 8])
            blocks.append(jnp.zeros((16, waves), F32))
        returned = jnp.concatenate(blocks, 0).astype(BF16)
        stage_back[pl.ds(t, waves, stride=2)] = dot_rows(unit(waves), returned)

    arrived(0, a_in)
    stage[...] = a_in[...].astype(F32).reshape(stage.shape)
    for t in range(2):
        grid_pair(t)
    b_out[...] = stage_back[...].astype(BF16).reshape(b_out.shape)
    push_ring(3, b_out, b_in, d_away, others_here)
    pltpu.make_async_copy(b_out.at[me], b_in.at[me], recv_sem.at[3]).start()

    target = iota((1, lat_all), 1)
    line = iota((lat_all // 2, lat_all), 0)
    for low in range(2):
        pick_rows = jnp.where(target == 2 * line + low, 1.0, 0.0).astype(BF16)
        lp[low] = dot(pick_rows, leg[...]).astype(BF16)

    degree = iota((1, trunc), 1).astype(F32)
    growth = degree * (degree + 1.0) / float(trunc * trunc)
    at_mode = iota((levels_all, LANES), 0)
    rates = jnp.zeros((levels_all, LANES), F32)
    for k in range(levels_all):
        rates = jnp.where(at_mode == k, rates_s[k], rates)
    inv[...] = 1.0 / (1.0 + rates[:, 0:1] * growth)

    arrived(4, v_in)
    whole = v_in[...].reshape(levels_all, LANES)
    whole_high = whole.astype(BF16).astype(F32)
    whole_low = whole - whole_high
    into = dot_rows(unit(LANES), jnp.concatenate([whole_high, whole_low], 0).astype(BF16))
    into = jnp.concatenate([into[0:levels_all, 0:levels_all], into[0:levels_all, levels_all:]], 0)
    into = jnp.concatenate([into, into], 1).astype(BF16)
    whole = vout_ref[...]
    whole_high = whole.astype(BF16).astype(F32)
    onto = jnp.concatenate([whole_high, whole - whole_high], 0)
    onto = jnp.concatenate([onto, onto], 1).astype(BF16)

    def place_rows(begin, value):
        for a in range(trunc // LANES):
            out32[a, pl.ds(begin, LEVS, stride=6)] = value[:, a * LANES : (a + 1) * LANES]

    def high_low(value):
        high = value.astype(BF16)
        low = (value - high.astype(F32)).astype(BF16)
        return jnp.concatenate([high, low], 0)

    def times(twice, value):
        both = dot(twice, high_low(value))
        return both[: both.shape[0] // 2] + both[both.shape[0] // 2 :]

    arrived(3, b_in)
    back = dot_rows(unit(LANES), b_in[...].reshape(lat_all // 2, LANES)).astype(BF16)
    for low in range(2):
        y_out[low] = back[low * HALF : low * HALF + 16]
        send(5 + low, lambda slot, low=low: y_out.at[low], y_in.at[low], y, y_peers)
    others = dot(back[16:48], lp[0]) + dot(back[HALF + 16 : HALF + 48], lp[1])
    others = jnp.where(kept, others, 0.0)
    for f in (1, 2):
        for part in range(2):
            begin = (f - 1) * 16 + part * 8
            place_rows(2 * f + part, others[begin : begin + LEVS])

    arrived(5, y_in.at[0])
    diverg = dot(y_in[0].reshape(ys * 16, lat_all // 2), lp[0])
    arrived(6, y_in.at[1])
    diverg = diverg + dot(y_in[1].reshape(ys * 16, lat_all // 2), lp[1])
    diverg = jnp.where(kept, diverg, 0.0)
    for part in range(2):
        of_part = [diverg[k * 16 + part * 8 : k * 16 + part * 8 + 8] for k in range(ys)]
        modes = times(into, jnp.concatenate(of_part, 0))
        solved = times(onto, modes * inv[...])
        place_rows(part, solved)
    for a in range(trunc // LANES):
        out_ref[0, :, a * LANES : (a + 1) * LANES] = out32[a].astype(BF16)

    sent(0, a_in, waves - 1)
    sent(3, b_in, waves - 1)
    sent(4, v_in, ys - 1)
    sent(5, y_in.at[0], ys - 1)
    sent(6, y_in.at[1], ys - 1)


def body(spec_in, legendre, wavenum, counts, quad_weights, vert_in, vert_out, mode_rates, zs, ys):
    _, columns, trunc = spec_in.shape
    ds = XS * CORES
    waves = ds * zs
    lat_all = waves * LATS
    levels_all = ys * LEVS
    points = -(-(PTS // 4 + 1) // LANES) * LANES
    any_place = pl.BlockSpec(memory_space=pl.ANY)
    return pl.pallas_call(
        functools.partial(kernel, zs, ys),
        out_shape=pltpu.VMEM((1, columns, trunc), BF16),
        in_specs=[any_place] * 9,
        out_specs=pl.BlockSpec(memory_space=pltpu.VMEM),
        scratch_shapes=[
            pltpu.VMEM((columns, trunc), BF16),
            pltpu.VMEM((1, waves), jnp.int32),
            pltpu.VMEM((LEVS, levels_all), F32),
            pltpu.VMEM((LEVS, levels_all), F32),
            pltpu.SMEM((waves,), jnp.int32),
            pltpu.SMEM((LATS,), jnp.int32),
            pltpu.SMEM((LATS,), F32),
            pltpu.SMEM((levels_all,), F32),
            pltpu.VMEM((lat_all, trunc), BF16),
            pltpu.VMEM((LANES, trunc), BF16),
            pltpu.VMEM((lat_all, LANES), F32),
            pltpu.VMEM((lat_all // 2, LANES), F32),
            pltpu.VMEM((lat_all // 2, LANES), F32),
            pltpu.VMEM((waves, LANES), F32),
            pltpu.VMEM((LATS, 2 * waves, points), BF16),
            pltpu.VMEM((LATS, points, 2 * waves), BF16),
            pltpu.VMEM((2, lat_all // 2, trunc), BF16),
            pltpu.VMEM((levels_all, trunc), F32),
            pltpu.VMEM((trunc // LANES, columns, LANES), F32),
            pltpu.VMEM((waves, 2, LANES), BF16),
            pltpu.VMEM((waves, 2, LANES), BF16),
            pltpu.VMEM((waves, 2, LANES), BF16),
            pltpu.VMEM((waves, 2, LANES), BF16),
            pltpu.VMEM((2, 16, lat_all // 2), BF16),
            pltpu.VMEM((2, ys, 16, lat_all // 2), BF16),
            pltpu.VMEM((LEVS, LANES), F32),
            pltpu.VMEM((ys, LEVS, LANES), F32),
            pltpu.SemaphoreType.DMA((8,)),
            pltpu.SemaphoreType.DMA((XS,)),
            pltpu.SemaphoreType.DMA((7,)),
            pltpu.SemaphoreType.DMA((7,)),
            pltpu.SemaphoreType.REGULAR,
        ],
        compiler_params=pltpu.CompilerParams(
            collective_id=0, has_side_effects=True, vmem_limit_bytes=60 * 1024 * 1024
        ),
    )(
        spec_in, legendre, wavenum, wavenum.reshape(1, -1), counts, quad_weights, mode_rates,
        vert_in.T, vert_out,
    )


def solution(mesh):
    zs = mesh.shape["lat"] // (XS * CORES)
    return jax.shard_map(
        functools.partial(body, zs=zs, ys=mesh.shape["lev"]),
        mesh=mesh,
        in_specs=(
            P("lat", "lev", None),
            P("lat", None, None),
            P(),
            P("lat"),
            P("lat"),
            P(None, "lev"),
            P("lev", None),
            P(),
        ),
        out_specs=P("lat", "lev", None),
        check_vma=False,
    )
```

```python
import functools
import math

import jax
import jax.numpy as jnp
from jax import lax
from jax.experimental import pallas as pl
from jax.experimental.pallas import tpu as pltpu
from jax.sharding import PartitionSpec as P

PTS = 5136
FIELDS = 3
XS = 4
CORES = 2
LATS = 4
LEVS = 8
LANES = 128
HALF = 64

F32 = jnp.float32
BF16 = jnp.bfloat16
MESH = pl.DeviceIdType.MESH

ROWS_BY_ROWS = (((1,), (1,)), ((), ()))


def dot(a, b):
    return jnp.dot(a, b, preferred_element_type=F32)


def dot_rows(a, b):
    return lax.dot_general(a, b, ROWS_BY_ROWS, preferred_element_type=F32)


def iota(shape, dim):
    return lax.broadcasted_iota(jnp.int32, shape, dim)


def unit(size):
    return jnp.where(iota((size, size), 0) == iota((size, size), 1), 1.0, 0.0).astype(BF16)


def half_up(value):
    return jnp.floor(value + 0.5)


def turn(steps, count, per_count):
    left = steps - half_up(steps * per_count) * count
    x = left * per_count * math.pi
    y = x * x
    s = -1.0 / 39916800
    for term in (1.0 / 362880, -1.0 / 5040, 1.0 / 120, -1.0 / 6, 1.0):
        s = s * y + term
    s = s * x
    c = 1.0 / 479001600
    for term in (-1.0 / 3628800, 1.0 / 40320, -1.0 / 720, 1.0 / 24, -0.5, 1.0):
        c = c * y + term
    return 1.0 - 2.0 * s * s, 2.0 * s * c


def kernel(
    zs, ys, spec_hbm, leg_hbm, wav_hbm, wav_row_hbm, counts_hbm, weights_hbm, rates_hbm, vin_hbm, vout_hbm,
    out_ref,
    spec_ref, wav_row, vin_ref, vout_ref, wav_s, counts_s, weights_s, rates_s,
    leg, spec2, fou, stage, stage_back, wcol, table, table_back, lp, inv, out32,
    a_out, a_in, b_out, b_in, y_out, y_in, v_out, v_in,
    load_sem, leg_sem, send_sem, recv_sem, all_in,
):
    ds = XS * CORES
    waves = ds * zs
    lat_all = waves * LATS
    trunc = spec_ref.shape[1]
    points = table.shape[2]
    levels_all = ys * LEVS
    me = lax.axis_index("lat")
    y = lax.axis_index("lev")
    x = me // (zs * CORES)
    z = (me // CORES) % zs
    core = me % CORES
    d = x * CORES + core

    def device(to_x, to_z, to_core):
        return (to_x * (zs * CORES) + to_z * CORES + to_core, y)

    def ring_away(i):
        odd = i % 2
        return odd * (zs // 2 - (i + 1) // 2) + (1 - odd) * (zs // 2 + i // 2)

    z_peers = []
    for i in range(zs - 1):
        to = (z + ring_away(i)) % zs
        z_peers.append((to, device(x, to, core)))
    d_away = [(k, c) for k in sorted(range(XS), key=lambda k: -min(k, XS - k)) for c in range(CORES)]
    d_peers = []
    for k, c in d_away:
        to_x, to_core = (x + k) % XS, (core + c) % CORES
        if (k, c) != (0, 0):
            d_peers.append((to_x * CORES + to_core, device(to_x, z, to_core)))
    y_peers = []
    for k in sorted(range(1, ys), key=lambda k: -min(k, ys - k)):
        to = (y + k) % ys
        y_peers.append((to, (me, to)))

    barrier = pltpu.get_barrier_semaphore()
    for _, to in z_peers + d_peers + y_peers:
        pl.semaphore_signal(barrier, inc=1, device_id=to, device_id_type=MESH)

    loads = []
    for source, target in (
        (spec_hbm.at[0], spec_ref), (wav_hbm, wav_s), (counts_hbm, counts_s), (weights_hbm, weights_s),
        (rates_hbm, rates_s), (wav_row_hbm, wav_row), (vin_hbm, vin_ref), (vout_hbm, vout_ref),
    ):
        loads.append(pltpu.make_async_copy(source, target, load_sem.at[len(loads)]))
        loads[-1].start()
    part_rows = lat_all // XS
    leg_loads = []
    for k in range(XS):
        rows = pl.ds(k * part_rows, part_rows)
        leg_loads.append(pltpu.make_async_copy(leg_hbm.at[0, rows], leg.at[rows], leg_sem.at[k]))
        leg_loads[-1].start()

    def send(number, source, arrive, slot, peers):
        pltpu.make_async_copy(source(slot), arrive.at[slot], recv_sem.at[number]).start()
        for to, to_device in peers:
            pltpu.make_async_remote_copy(
                src_ref=source(to), dst_ref=arrive.at[slot],
                send_sem=send_sem.at[number], recv_sem=recv_sem.at[number],
                device_id=to_device, device_id_type=MESH,
            ).start()

    def arrived(number, arrive):
        pltpu.make_async_copy(arrive, arrive, recv_sem.at[number]).wait()

    def sent(number, arrive, count):
        part = arrive.at[pl.ds(0, count)]
        pltpu.make_async_copy(part, part, send_sem.at[number]).wait()

    loads[0].wait()
    loads[1].wait()
    order = wav_s[me]
    kept = iota((1, trunc), 1) >= order
    columns = spec_ref.shape[0]
    masked = jnp.where(kept, spec_ref[...].astype(F32), 0.0).astype(BF16)
    blank = jnp.zeros((HALF - columns, trunc), BF16)
    spec2[0:columns] = masked
    spec2[columns:HALF] = blank
    spec2[HALF : HALF + columns] = masked
    spec2[HALF + columns :] = blank

    for k in range(XS):
        leg_loads[k].wait()
        rows = pl.ds(k * part_rows, part_rows)
        fou[rows] = dot_rows(leg[rows], spec2[...])
    first_half = iota((lat_all // 2, LANES), 1) < HALF
    low = fou[pl.ds(0, lat_all // 2, stride=2)]
    high = fou[pl.ds(1, lat_all // 2, stride=2)]
    a_out[...] = jnp.where(first_half, low, high).astype(BF16).reshape(a_out.shape)

    def push(number, leave, arrive, to_x, to_z, to_core):
        to = device(to_x, to_z, to_core)
        pltpu.make_async_remote_copy(
            src_ref=leave.at[to[0]], dst_ref=arrive.at[me],
            send_sem=send_sem.at[number], recv_sem=recv_sem.at[number],
            device_id=to, device_id_type=MESH,
        ).start()

    def push_ring(number, leave, arrive, pairs, own):
        def push_pairs(away, some):
            for k, c in some:
                push(number, leave, arrive, (x + k) % XS, (z + away) % zs, (core + c) % CORES)

        def one(i, carry):
            push_pairs(ring_away(i), pairs)
            return carry

        lax.fori_loop(0, zs - 1, one, 0)
        push_pairs(0, own)

    others_here = [pair for pair in d_away if pair != (0, 0)]

    pl.semaphore_wait(barrier, len(z_peers) + len(d_peers) + len(y_peers))
    for _, to in d_peers:
        pl.semaphore_signal(all_in, inc=1, device_id=to, device_id_type=MESH)
    push_ring(0, a_out, a_in, [(0, 0)], [])
    pltpu.make_async_copy(a_out.at[me], a_in.at[me], recv_sem.at[0]).start()
    pl.semaphore_wait(all_in, len(d_peers))
    push_ring(0, a_out, a_in, others_here, others_here)

    for load in loads[2:]:
        load.wait()

    v_out[...] = jnp.zeros(v_out.shape, F32)
    v_out[:, 0:levels_all] = vin_ref[...]
    send(4, lambda slot: v_out, v_in, y, y_peers)

    place = iota((waves, waves), 0)
    across = iota((waves, waves), 1)
    row = wav_row[...].astype(F32)
    even = row - 2.0 * jnp.floor(row * 0.5) == 0.0
    parity = jnp.where(even, 1.0, -1.0)
    column = jnp.sum(jnp.where(across == place, row, 0.0), axis=1, keepdims=True)
    wcol[...] = jnp.broadcast_to(column, wcol.shape)

    def table_part(step, carry):
        lat = step // 4
        chunk = waves // 4
        begin = pl.multiple_of((step % 4) * chunk, chunk)
        count = jnp.full((chunk, LANES), counts_s[lat].astype(F32), F32)
        per_count = 1.0 / count
        waves_here = wcol[pl.ds(begin, chunk)]
        offset = iota((chunk, LANES), 1).astype(F32)
        c, s = turn(waves_here * offset, count, per_count)
        step_c, step_s = turn(waves_here * float(LANES), count, per_count)
        for a in range(points // LANES):
            at = slice(a * LANES, (a + 1) * LANES)
            table[lat, pl.ds(begin, chunk), at] = c.astype(BF16)
            table[lat, pl.ds(waves + begin, chunk), at] = s.astype(BF16)
            c, s = c * step_c - s * step_s, s * step_c + c * step_s
        return carry

    lax.fori_loop(0, LATS * 4, table_part, 0)

    def back_part(step, carry):
        lat = step // 4
        chunk = LANES // 4
        begin = pl.multiple_of((step % 4) * chunk, chunk)
        count = jnp.full((chunk, waves), counts_s[lat].astype(F32), F32)
        per_count = 1.0 / count
        quarter = counts_s[lat] // 4
        offset = (iota((chunk, waves), 0) + begin).astype(F32)
        c, s = turn(row * offset, count, per_count)
        step_c, step_s = turn(jnp.broadcast_to(row * float(LANES), (chunk, waves)), count, per_count)
        for a in range(points // LANES):
            at = pl.ds(a * LANES + begin, chunk)
            j = iota((chunk, waves), 0) + (a * LANES + begin)
            share = jnp.where((j == 0) | (j == quarter), 0.5, jnp.where(j > quarter, 0.0, 1.0))
            table_back[lat, at, 0:waves] = (c * share).astype(BF16)
            table_back[lat, at, waves:] = (s * share).astype(BF16)
            c, s = c * step_c - s * step_s, s * step_c + c * step_s
        return carry

    lax.fori_loop(0, LATS * 4, back_part, 0)

    r = iota((LANES, LANES), 0)
    field = (r // LEVS) % 4
    wanted = (r // HALF) * HALF + (r % LEVS) * 6 + 2 * field + (r // 32) % 2
    pick = jnp.where((iota((LANES, LANES), 1) == wanted) & (field < 3), 1.0, 0.0).astype(BF16)


    def synthesis(lat, coeffs):
        begin = (lat % 2) * HALF
        cosine = coeffs[begin : begin + 24]
        sine = coeffs[begin + 32 : begin + 56]
        turned = parity * cosine
        turned_sine = parity * sine
        w = jnp.concatenate(
            [
                jnp.concatenate([cosine, sine], 1),
                jnp.concatenate([cosine, -sine], 1),
                jnp.concatenate([turned, turned_sine], 1),
                jnp.concatenate([turned, -turned_sine], 1),
            ],
            0,
        ).astype(BF16)
        return dot(w, table[lat])

    def products(grid):
        tend = []
        for q in range(4):
            g = [grid[q * 24 + f * 8 : q * 24 + f * 8 + 8] for f in range(FIELDS)]
            tend.append([g[0] - g[1] * g[2], g[1] + g[0] * g[2], g[2] - g[0] * g[1]])
        folded = [[], [], [], []]
        for f in range(FIELDS):
            t0, t1, t2, t3 = (tend[q][f] for q in range(4))
            plus, minus = t0 + t1, t0 - t1
            plus_far, minus_far = t2 + t3, t2 - t3
            folded[0].append(plus + plus_far)
            folded[1].append(plus - plus_far)
            folded[2].append(minus + minus_far)
            folded[3].append(minus - minus_far)
        return jnp.concatenate(folded[0] + folded[1] + folded[2] + folded[3], 0).astype(BF16)

    def analysis(lat, u):
        back = dot(u, table_back[lat])
        count_f = jnp.full((1, waves), counts_s[lat].astype(F32), F32)
        factor = jnp.full((1, waves), weights_s[lat], F32) / jnp.sqrt(count_f)
        cos_out = jnp.where(even, back[0:24, :waves], back[24:48, :waves]) * factor
        sin_out = jnp.where(even, back[48:72, waves:], back[72:96, waves:]) * -factor
        blocks = []
        for f in range(FIELDS):
            blocks.append(cos_out[f * 8 : f * 8 + 8])
            blocks.append(sin_out[f * 8 : f * 8 + 8])
        return blocks + [jnp.zeros((16, waves), F32)]

    arrived(0, a_in)
    stage[...] = a_in[...].astype(F32).reshape(stage.shape)
    coeffs = []
    for t in range(2):
        got = stage[pl.ds(t, waves, stride=2)].astype(BF16)
        coeffs.append(dot_rows(pick, got) * (1.0 / math.sqrt(2 * waves)))
    grids = [synthesis(lat, coeffs[lat // 2]) for lat in range(LATS)]
    folds = [products(grid) for grid in grids]
    blocks = [analysis(lat, folds[lat]) for lat in range(LATS)]
    for t in range(2):
        returned = jnp.concatenate(blocks[2 * t] + blocks[2 * t + 1], 0).astype(BF16)
        stage_back[pl.ds(t, waves, stride=2)] = dot_rows(unit(waves), returned)
    b_out[...] = stage_back[...].astype(BF16).reshape(b_out.shape)
    push_ring(3, b_out, b_in, d_away, others_here)
    pltpu.make_async_copy(b_out.at[me], b_in.at[me], recv_sem.at[3]).start()

    target = iota((1, lat_all), 1)
    line = iota((lat_all // 2, lat_all), 0)
    for low in range(2):
        pick_rows = jnp.where(target == 2 * line + low, 1.0, 0.0).astype(BF16)
        lp[low * (lat_all // 2) : (low + 1) * (lat_all // 2)] = dot(pick_rows, leg[...]).astype(BF16)

    degree = iota((1, trunc), 1).astype(F32)
    growth = degree * (degree + 1.0) / float(trunc * trunc)
    at_mode = iota((levels_all, LANES), 0)
    rates = jnp.zeros((levels_all, LANES), F32)
    for k in range(levels_all):
        rates = jnp.where(at_mode == k, rates_s[k], rates)
    inv[...] = 1.0 / (1.0 + rates[:, 0:1] * growth)

    arrived(4, v_in)
    whole = v_in[...].reshape(levels_all, LANES)
    whole_high = whole.astype(BF16).astype(F32)
    whole_low = whole - whole_high
    into = dot_rows(unit(LANES), jnp.concatenate([whole_high, whole_low], 0).astype(BF16))
    into = jnp.concatenate([into[0:levels_all, 0:levels_all], into[0:levels_all, levels_all:]], 0)
    into = jnp.concatenate([into, into], 1).astype(BF16)
    whole = vout_ref[...]
    whole_high = whole.astype(BF16).astype(F32)
    onto = jnp.concatenate([whole_high, whole - whole_high], 0)
    onto = jnp.concatenate([onto, onto], 1).astype(BF16)

    def place_rows(begin, value):
        for a in range(trunc // LANES):
            out32[a, pl.ds(begin, LEVS, stride=6)] = value[:, a * LANES : (a + 1) * LANES]

    def high_low(value):
        high = value.astype(BF16)
        low = (value - high.astype(F32)).astype(BF16)
        return jnp.concatenate([high, low], 0)

    def times(twice, value):
        both = dot(twice, high_low(value))
        return both[: both.shape[0] // 2] + both[both.shape[0] // 2 :]

    arrived(3, b_in)
    back = dot_rows(unit(LANES), b_in[...].reshape(lat_all // 2, LANES)).astype(BF16)
    y_out[:, 0 : lat_all // 2] = back[0:16]
    y_out[:, lat_all // 2 :] = back[HALF : HALF + 16]
    send(5, lambda slot: y_out, y_in, y, y_peers)
    others = dot(jnp.concatenate([back[16:48], back[HALF + 16 : HALF + 48]], 1), lp[...])
    others = jnp.where(kept, others, 0.0)
    for f in (1, 2):
        for part in range(2):
            begin = (f - 1) * 16 + part * 8
            place_rows(2 * f + part, others[begin : begin + LEVS])

    arrived(5, y_in)
    diverg = dot(y_in[...].reshape(ys * 16, lat_all), lp[...])
    diverg = jnp.where(kept, diverg, 0.0)
    levels = [
        jnp.concatenate([diverg[k * 16 + part * 8 : k * 16 + part * 8 + 8] for k in range(ys)], 0)
        for part in range(2)
    ]
    modes = [times(into, value) for value in levels]
    solved = [times(onto, value * inv[...]) for value in modes]
    for part in range(2):
        place_rows(part, solved[part])
    for a in range(trunc // LANES):
        out_ref[0, :, a * LANES : (a + 1) * LANES] = out32[a].astype(BF16)

    sent(0, a_in, waves - 1)
    sent(3, b_in, waves - 1)
    sent(4, v_in, ys - 1)
    sent(5, y_in, ys - 1)


def body(spec_in, legendre, wavenum, counts, quad_weights, vert_in, vert_out, mode_rates, zs, ys):
    _, columns, trunc = spec_in.shape
    ds = XS * CORES
    waves = ds * zs
    lat_all = waves * LATS
    levels_all = ys * LEVS
    points = -(-(PTS // 4 + 1) // LANES) * LANES
    any_place = pl.BlockSpec(memory_space=pl.ANY)
    return pl.pallas_call(
        functools.partial(kernel, zs, ys),
        out_shape=pltpu.VMEM((1, columns, trunc), BF16),
        in_specs=[any_place] * 9,
        out_specs=pl.BlockSpec(memory_space=pltpu.VMEM),
        scratch_shapes=[
            pltpu.VMEM((columns, trunc), BF16),
            pltpu.VMEM((1, waves), jnp.int32),
            pltpu.VMEM((LEVS, levels_all), F32),
            pltpu.VMEM((LEVS, levels_all), F32),
            pltpu.SMEM((waves,), jnp.int32),
            pltpu.SMEM((LATS,), jnp.int32),
            pltpu.SMEM((LATS,), F32),
            pltpu.SMEM((levels_all,), F32),
            pltpu.VMEM((lat_all, trunc), BF16),
            pltpu.VMEM((LANES, trunc), BF16),
            pltpu.VMEM((lat_all, LANES), F32),
            pltpu.VMEM((lat_all // 2, LANES), F32),
            pltpu.VMEM((lat_all // 2, LANES), F32),
            pltpu.VMEM((waves, LANES), F32),
            pltpu.VMEM((LATS, 2 * waves, points), BF16),
            pltpu.VMEM((LATS, points, 2 * waves), BF16),
            pltpu.VMEM((lat_all, trunc), BF16),
            pltpu.VMEM((levels_all, trunc), F32),
            pltpu.VMEM((trunc // LANES, columns, LANES), F32),
            pltpu.VMEM((waves, 2, LANES), BF16),
            pltpu.VMEM((waves, 2, LANES), BF16),
            pltpu.VMEM((waves, 2, LANES), BF16),
            pltpu.VMEM((waves, 2, LANES), BF16),
            pltpu.VMEM((16, lat_all), BF16),
            pltpu.VMEM((ys, 16, lat_all), BF16),
            pltpu.VMEM((LEVS, LANES), F32),
            pltpu.VMEM((ys, LEVS, LANES), F32),
            pltpu.SemaphoreType.DMA((8,)),
            pltpu.SemaphoreType.DMA((XS,)),
            pltpu.SemaphoreType.DMA((7,)),
            pltpu.SemaphoreType.DMA((7,)),
            pltpu.SemaphoreType.REGULAR,
        ],
        compiler_params=pltpu.CompilerParams(
            collective_id=0, has_side_effects=True, vmem_limit_bytes=60 * 1024 * 1024
        ),
    )(
        spec_in, legendre, wavenum, wavenum.reshape(1, -1), counts, quad_weights, mode_rates,
        vert_in.T, vert_out,
    )


def solution(mesh):
    zs = mesh.shape["lat"] // (XS * CORES)
    return jax.shard_map(
        functools.partial(body, zs=zs, ys=mesh.shape["lev"]),
        mesh=mesh,
        in_specs=(
            P("lat", "lev", None),
            P("lat", None, None),
            P(),
            P("lat"),
            P("lat"),
            P(None, "lev"),
            P("lev", None),
            P(),
        ),
        out_specs=P("lat", "lev", None),
        check_vma=False,
    )
```

```python
import functools
import math

import jax
import jax.numpy as jnp
from jax import lax
from jax.experimental import pallas as pl
from jax.experimental.pallas import tpu as pltpu
from jax.sharding import PartitionSpec as P

PTS = 5136
FIELDS = 3
XS = 4
CORES = 2
LATS = 4
LEVS = 8
LANES = 128
HALF = 64

F32 = jnp.float32
BF16 = jnp.bfloat16
MESH = pl.DeviceIdType.MESH

ROWS_BY_ROWS = (((1,), (1,)), ((), ()))


def dot(a, b):
    return jnp.dot(a, b, preferred_element_type=F32)


def dot_rows(a, b):
    return lax.dot_general(a, b, ROWS_BY_ROWS, preferred_element_type=F32)


def iota(shape, dim):
    return lax.broadcasted_iota(jnp.int32, shape, dim)


def unit(size):
    return jnp.where(iota((size, size), 0) == iota((size, size), 1), 1.0, 0.0).astype(BF16)


def half_up(value):
    return jnp.floor(value + 0.5)


def turn(steps, count, per_count):
    left = steps - half_up(steps * per_count) * count
    x = left * per_count * math.pi
    y = x * x
    s = -1.0 / 39916800
    for term in (1.0 / 362880, -1.0 / 5040, 1.0 / 120, -1.0 / 6, 1.0):
        s = s * y + term
    s = s * x
    c = 1.0 / 479001600
    for term in (-1.0 / 3628800, 1.0 / 40320, -1.0 / 720, 1.0 / 24, -0.5, 1.0):
        c = c * y + term
    return 1.0 - 2.0 * s * s, 2.0 * s * c


def kernel(
    zs, ys, spec_hbm, leg_hbm, wav_hbm, wav_row_hbm, counts_hbm, weights_hbm, rates_hbm, vin_hbm, vout_hbm,
    out_ref,
    spec_ref, wav_row, vin_ref, vout_ref, wav_s, counts_s, weights_s, rates_s,
    leg, spec2, fou, stage, stage_back, wcol, table, table_back, lp, inv, out32,
    a_out, a_in, b_out, b_in, y_out, y_in, v_out, v_in,
    load_sem, leg_sem, send_sem, recv_sem, all_in,
):
    ds = XS * CORES
    waves = ds * zs
    lat_all = waves * LATS
    trunc = spec_ref.shape[1]
    points = table.shape[2]
    levels_all = ys * LEVS
    me = lax.axis_index("lat")
    y = lax.axis_index("lev")
    x = me // (zs * CORES)
    z = (me // CORES) % zs
    core = me % CORES
    d = x * CORES + core

    def device(to_x, to_z, to_core):
        return (to_x * (zs * CORES) + to_z * CORES + to_core, y)

    def ring_away(i):
        odd = i % 2
        return odd * (zs // 2 - (i + 1) // 2) + (1 - odd) * (zs // 2 + i // 2)

    z_peers = []
    for i in range(zs - 1):
        to = (z + ring_away(i)) % zs
        z_peers.append((to, device(x, to, core)))
    d_away = [(k, c) for k in sorted(range(XS), key=lambda k: -min(k, XS - k)) for c in range(CORES)]
    d_peers = []
    for k, c in d_away:
        to_x, to_core = (x + k) % XS, (core + c) % CORES
        if (k, c) != (0, 0):
            d_peers.append((to_x * CORES + to_core, device(to_x, z, to_core)))
    y_peers = []
    for k in sorted(range(1, ys), key=lambda k: -min(k, ys - k)):
        to = (y + k) % ys
        y_peers.append((to, (me, to)))

    barrier = pltpu.get_barrier_semaphore()
    for _, to in z_peers + d_peers + y_peers:
        pl.semaphore_signal(barrier, inc=1, device_id=to, device_id_type=MESH)

    loads = []
    for source, target in (
        (spec_hbm.at[0], spec_ref), (wav_hbm, wav_s), (counts_hbm, counts_s), (weights_hbm, weights_s),
        (rates_hbm, rates_s), (wav_row_hbm, wav_row), (vin_hbm, vin_ref), (vout_hbm, vout_ref),
    ):
        loads.append(pltpu.make_async_copy(source, target, load_sem.at[len(loads)]))
        loads[-1].start()
    part_rows = lat_all // XS
    leg_loads = []
    for k in range(XS):
        rows = pl.ds(k * part_rows, part_rows)
        leg_loads.append(pltpu.make_async_copy(leg_hbm.at[0, rows], leg.at[rows], leg_sem.at[k]))
        leg_loads[-1].start()

    def send(number, source, arrive, slot, peers):
        pltpu.make_async_copy(source(slot), arrive.at[slot], recv_sem.at[number]).start()
        for to, to_device in peers:
            pltpu.make_async_remote_copy(
                src_ref=source(to), dst_ref=arrive.at[slot],
                send_sem=send_sem.at[number], recv_sem=recv_sem.at[number],
                device_id=to_device, device_id_type=MESH,
            ).start()

    def arrived(number, arrive):
        pltpu.make_async_copy(arrive, arrive, recv_sem.at[number]).wait()

    def sent(number, arrive, count):
        part = arrive.at[pl.ds(0, count)]
        pltpu.make_async_copy(part, part, send_sem.at[number]).wait()

    loads[0].wait()
    loads[1].wait()
    order = wav_s[me]
    kept = iota((1, trunc), 1) >= order
    columns = spec_ref.shape[0]
    masked = jnp.where(kept, spec_ref[...].astype(F32), 0.0).astype(BF16)
    blank = jnp.zeros((HALF - columns, trunc), BF16)
    spec2[0:columns] = masked
    spec2[columns:HALF] = blank
    spec2[HALF : HALF + columns] = masked
    spec2[HALF + columns :] = blank

    for k in range(XS):
        leg_loads[k].wait()
        rows = pl.ds(k * part_rows, part_rows)
        fou[rows] = dot_rows(leg[rows], spec2[...])
    first_half = iota((lat_all // 2, LANES), 1) < HALF
    low = fou[pl.ds(0, lat_all // 2, stride=2)]
    high = fou[pl.ds(1, lat_all // 2, stride=2)]
    a_out[...] = jnp.where(first_half, low, high).astype(BF16).reshape(a_out.shape)

    def push(number, leave, arrive, to_x, to_z, to_core):
        to = device(to_x, to_z, to_core)
        pltpu.make_async_remote_copy(
            src_ref=leave.at[to[0]], dst_ref=arrive.at[me],
            send_sem=send_sem.at[number], recv_sem=recv_sem.at[number],
            device_id=to, device_id_type=MESH,
        ).start()

    def push_ring(number, leave, arrive, pairs, own):
        def push_pairs(away, some):
            for k, c in some:
                push(number, leave, arrive, (x + k) % XS, (z + away) % zs, (core + c) % CORES)

        def one(i, carry):
            push_pairs(ring_away(i), pairs)
            return carry

        lax.fori_loop(0, zs - 1, one, 0)
        push_pairs(0, own)

    others_here = [pair for pair in d_away if pair != (0, 0)]

    pl.semaphore_wait(barrier, len(z_peers) + len(d_peers) + len(y_peers))
    for _, to in d_peers:
        pl.semaphore_signal(all_in, inc=1, device_id=to, device_id_type=MESH)
    push_ring(0, a_out, a_in, [(0, 0)], [])
    pltpu.make_async_copy(a_out.at[me], a_in.at[me], recv_sem.at[0]).start()
    pl.semaphore_wait(all_in, len(d_peers))
    push_ring(0, a_out, a_in, others_here, others_here)

    for load in loads[2:]:
        load.wait()

    v_out[...] = jnp.zeros(v_out.shape, F32)
    v_out[:, 0:levels_all] = vin_ref[...]
    send(4, lambda slot: v_out, v_in, y, y_peers)

    place = iota((waves, waves), 0)
    across = iota((waves, waves), 1)
    row = wav_row[...].astype(F32)
    even = row - 2.0 * jnp.floor(row * 0.5) == 0.0
    parity = jnp.where(even, 1.0, -1.0)
    column = jnp.sum(jnp.where(across == place, row, 0.0), axis=1, keepdims=True)
    wcol[...] = jnp.broadcast_to(column, wcol.shape)

    def table_part(step, carry):
        lat = step // 4
        chunk = waves // 4
        begin = pl.multiple_of((step % 4) * chunk, chunk)
        count = jnp.full((chunk, LANES), counts_s[lat].astype(F32), F32)
        per_count = 1.0 / count
        waves_here = wcol[pl.ds(begin, chunk)]
        offset = iota((chunk, LANES), 1).astype(F32)
        c, s = turn(waves_here * offset, count, per_count)
        step_c, step_s = turn(waves_here * float(LANES), count, per_count)
        for a in range(points // LANES):
            at = slice(a * LANES, (a + 1) * LANES)
            table[lat, pl.ds(begin, chunk), at] = c.astype(BF16)
            table[lat, pl.ds(waves + begin, chunk), at] = s.astype(BF16)
            c, s = c * step_c - s * step_s, s * step_c + c * step_s
        return carry

    lax.fori_loop(0, LATS * 4, table_part, 0)

    def back_part(step, carry):
        lat = step // 4
        chunk = LANES // 4
        begin = pl.multiple_of((step % 4) * chunk, chunk)
        count = jnp.full((chunk, waves), counts_s[lat].astype(F32), F32)
        per_count = 1.0 / count
        quarter = counts_s[lat] // 4
        offset = (iota((chunk, waves), 0) + begin).astype(F32)
        c, s = turn(row * offset, count, per_count)
        step_c, step_s = turn(jnp.broadcast_to(row * float(LANES), (chunk, waves)), count, per_count)
        for a in range(points // LANES):
            at = pl.ds(a * LANES + begin, chunk)
            j = iota((chunk, waves), 0) + (a * LANES + begin)
            share = jnp.where((j == 0) | (j == quarter), 0.5, jnp.where(j > quarter, 0.0, 1.0))
            table_back[lat, at, 0:waves] = (c * share).astype(BF16)
            table_back[lat, at, waves:] = (s * share).astype(BF16)
            c, s = c * step_c - s * step_s, s * step_c + c * step_s
        return carry

    lax.fori_loop(0, LATS * 4, back_part, 0)

    r = iota((LANES, LANES), 0)
    field = (r // LEVS) % 4
    wanted = (r // HALF) * HALF + (r % LEVS) * 6 + 2 * field + (r // 32) % 2
    pick = jnp.where((iota((LANES, LANES), 1) == wanted) & (field < 3), 1.0, 0.0).astype(BF16)


    def synthesis(lat, coeffs):
        begin = (lat % 2) * HALF
        cosine = coeffs[begin : begin + 24]
        sine = coeffs[begin + 32 : begin + 56]
        turned = parity * cosine
        turned_sine = parity * sine
        w = jnp.concatenate(
            [
                jnp.concatenate([cosine, sine], 1),
                jnp.concatenate([cosine, -sine], 1),
                jnp.concatenate([turned, turned_sine], 1),
                jnp.concatenate([turned, -turned_sine], 1),
            ],
            0,
        ).astype(BF16)
        return dot(w, table[lat])

    def products(grid):
        tend = []
        for q in range(4):
            g = [grid[q * 24 + f * 8 : q * 24 + f * 8 + 8] for f in range(FIELDS)]
            tend.append([g[0] - g[1] * g[2], g[1] + g[0] * g[2], g[2] - g[0] * g[1]])
        folded = [[], [], [], []]
        for f in range(FIELDS):
            t0, t1, t2, t3 = (tend[q][f] for q in range(4))
            plus, minus = t0 + t1, t0 - t1
            plus_far, minus_far = t2 + t3, t2 - t3
            folded[0].append(plus + plus_far)
            folded[1].append(plus - plus_far)
            folded[2].append(minus + minus_far)
            folded[3].append(minus - minus_far)
        return jnp.concatenate(folded[0] + folded[1] + folded[2] + folded[3], 0).astype(BF16)

    def analysis(lat, u):
        back = dot(u, table_back[lat])
        count_f = jnp.full((1, waves), counts_s[lat].astype(F32), F32)
        factor = jnp.full((1, waves), weights_s[lat], F32) / jnp.sqrt(count_f)
        cos_out = jnp.where(even, back[0:24, :waves], back[24:48, :waves]) * factor
        sin_out = jnp.where(even, back[48:72, waves:], back[72:96, waves:]) * -factor
        blocks = []
        for f in range(FIELDS):
            blocks.append(cos_out[f * 8 : f * 8 + 8])
            blocks.append(sin_out[f * 8 : f * 8 + 8])
        return blocks + [jnp.zeros((16, waves), F32)]

    arrived(0, a_in)
    stage[...] = a_in[...].astype(F32).reshape(stage.shape)
    got = [stage[pl.ds(t, waves, stride=2)] for t in range(2)]
    both = dot_rows(pick, jnp.concatenate(got, 0).astype(BF16)) * (1.0 / math.sqrt(2 * waves))
    coeffs = [both[:, :waves], both[:, waves:]]
    grids = [synthesis(lat, coeffs[lat // 2]) for lat in range(LATS)]
    folds = [products(grid) for grid in grids]
    blocks = [analysis(lat, folds[lat]) for lat in range(LATS)]
    returned = jnp.concatenate(blocks[0] + blocks[1] + blocks[2] + blocks[3], 0).astype(BF16)
    turned_back = dot_rows(unit(waves), returned)
    for t in range(2):
        stage_back[pl.ds(t, waves, stride=2)] = turned_back[:, t * LANES : (t + 1) * LANES]
    b_out[...] = stage_back[...].astype(BF16).reshape(b_out.shape)
    push_ring(3, b_out, b_in, d_away, others_here)
    pltpu.make_async_copy(b_out.at[me], b_in.at[me], recv_sem.at[3]).start()

    target = iota((1, lat_all), 1)
    line = iota((lat_all // 2, lat_all), 0)
    for low in range(2):
        pick_rows = jnp.where(target == 2 * line + low, 1.0, 0.0).astype(BF16)
        lp[low * (lat_all // 2) : (low + 1) * (lat_all // 2)] = dot(pick_rows, leg[...]).astype(BF16)

    degree = iota((1, trunc), 1).astype(F32)
    growth = degree * (degree + 1.0) / float(trunc * trunc)
    at_mode = iota((levels_all, LANES), 0)
    rates = jnp.zeros((levels_all, LANES), F32)
    for k in range(levels_all):
        rates = jnp.where(at_mode == k, rates_s[k], rates)
    inv[...] = 1.0 / (1.0 + rates[:, 0:1] * growth)

    arrived(4, v_in)
    whole = v_in[...].reshape(levels_all, LANES)
    whole_high = whole.astype(BF16).astype(F32)
    whole_low = whole - whole_high
    into = dot_rows(unit(LANES), jnp.concatenate([whole_high, whole_low], 0).astype(BF16))
    into = jnp.concatenate([into[0:levels_all, 0:levels_all], into[0:levels_all, levels_all:]], 0)
    into = jnp.concatenate([into, into], 1).astype(BF16)
    whole = vout_ref[...]
    whole_high = whole.astype(BF16).astype(F32)
    onto = jnp.concatenate([whole_high, whole - whole_high], 0)
    onto = jnp.concatenate([onto, onto], 1).astype(BF16)

    def place_rows(begin, value):
        for a in range(trunc // LANES):
            out32[a, pl.ds(begin, LEVS, stride=6)] = value[:, a * LANES : (a + 1) * LANES]

    def high_low(value):
        high = value.astype(BF16)
        low = (value - high.astype(F32)).astype(BF16)
        return jnp.concatenate([high, low], 0)

    def times(twice, value):
        both = dot(twice, high_low(value))
        return both[: both.shape[0] // 2] + both[both.shape[0] // 2 :]

    arrived(3, b_in)
    back = dot_rows(unit(LANES), b_in[...].reshape(lat_all // 2, LANES)).astype(BF16)
    y_out[:, 0 : lat_all // 2] = back[0:16]
    y_out[:, lat_all // 2 :] = back[HALF : HALF + 16]
    send(5, lambda slot: y_out, y_in, y, y_peers)
    others = dot(jnp.concatenate([back[16:48], back[HALF + 16 : HALF + 48]], 1), lp[...])
    others = jnp.where(kept, others, 0.0)
    for f in (1, 2):
        for part in range(2):
            begin = (f - 1) * 16 + part * 8
            place_rows(2 * f + part, others[begin : begin + LEVS])

    arrived(5, y_in)
    diverg = dot(y_in[...].reshape(ys * 16, lat_all), lp[...])
    diverg = jnp.where(kept, diverg, 0.0)
    levels = [
        jnp.concatenate([diverg[k * 16 + part * 8 : k * 16 + part * 8 + 8] for k in range(ys)], 0)
        for part in range(2)
    ]
    modes = [times(into, value) for value in levels]
    solved = [times(onto, value * inv[...]) for value in modes]
    for part in range(2):
        place_rows(part, solved[part])
    for a in range(trunc // LANES):
        out_ref[0, :, a * LANES : (a + 1) * LANES] = out32[a].astype(BF16)

    sent(0, a_in, waves - 1)
    sent(3, b_in, waves - 1)
    sent(4, v_in, ys - 1)
    sent(5, y_in, ys - 1)


def body(spec_in, legendre, wavenum, counts, quad_weights, vert_in, vert_out, mode_rates, zs, ys):
    _, columns, trunc = spec_in.shape
    ds = XS * CORES
    waves = ds * zs
    lat_all = waves * LATS
    levels_all = ys * LEVS
    points = -(-(PTS // 4 + 1) // LANES) * LANES
    any_place = pl.BlockSpec(memory_space=pl.ANY)
    return pl.pallas_call(
        functools.partial(kernel, zs, ys),
        out_shape=pltpu.VMEM((1, columns, trunc), BF16),
        in_specs=[any_place] * 9,
        out_specs=pl.BlockSpec(memory_space=pltpu.VMEM),
        scratch_shapes=[
            pltpu.VMEM((columns, trunc), BF16),
            pltpu.VMEM((1, waves), jnp.int32),
            pltpu.VMEM((LEVS, levels_all), F32),
            pltpu.VMEM((LEVS, levels_all), F32),
            pltpu.SMEM((waves,), jnp.int32),
            pltpu.SMEM((LATS,), jnp.int32),
            pltpu.SMEM((LATS,), F32),
            pltpu.SMEM((levels_all,), F32),
            pltpu.VMEM((lat_all, trunc), BF16),
            pltpu.VMEM((LANES, trunc), BF16),
            pltpu.VMEM((lat_all, LANES), F32),
            pltpu.VMEM((lat_all // 2, LANES), F32),
            pltpu.VMEM((lat_all // 2, LANES), F32),
            pltpu.VMEM((waves, LANES), F32),
            pltpu.VMEM((LATS, 2 * waves, points), BF16),
            pltpu.VMEM((LATS, points, 2 * waves), BF16),
            pltpu.VMEM((lat_all, trunc), BF16),
            pltpu.VMEM((levels_all, trunc), F32),
            pltpu.VMEM((trunc // LANES, columns, LANES), F32),
            pltpu.VMEM((waves, 2, LANES), BF16),
            pltpu.VMEM((waves, 2, LANES), BF16),
            pltpu.VMEM((waves, 2, LANES), BF16),
            pltpu.VMEM((waves, 2, LANES), BF16),
            pltpu.VMEM((16, lat_all), BF16),
            pltpu.VMEM((ys, 16, lat_all), BF16),
            pltpu.VMEM((LEVS, LANES), F32),
            pltpu.VMEM((ys, LEVS, LANES), F32),
            pltpu.SemaphoreType.DMA((8,)),
            pltpu.SemaphoreType.DMA((XS,)),
            pltpu.SemaphoreType.DMA((7,)),
            pltpu.SemaphoreType.DMA((7,)),
            pltpu.SemaphoreType.REGULAR,
        ],
        compiler_params=pltpu.CompilerParams(
            collective_id=0, has_side_effects=True, vmem_limit_bytes=60 * 1024 * 1024
        ),
    )(
        spec_in, legendre, wavenum, wavenum.reshape(1, -1), counts, quad_weights, mode_rates,
        vert_in.T, vert_out,
    )


def solution(mesh):
    zs = mesh.shape["lat"] // (XS * CORES)
    return jax.shard_map(
        functools.partial(body, zs=zs, ys=mesh.shape["lev"]),
        mesh=mesh,
        in_specs=(
            P("lat", "lev", None),
            P("lat", None, None),
            P(),
            P("lat"),
            P("lat"),
            P(None, "lev"),
            P("lev", None),
            P(),
        ),
        out_specs=P("lat", "lev", None),
        check_vma=False,
    )
```
